512 devices in a mesh: dest: 128 (over x, z, core), orig: 4 (over y).
Axes of the slice: x: 4, y: 4, z: 16, core: 2. Of those that a mesh axis runs over, the one named last changes fastest.
Arguments:
- zone_feat: bfloat16 [19, 65536], P(None, 'dest'), may hold values from -6 to 6
- anchor_zone: int32 [16], P('orig'), may hold values from 0 to 65535
- distance: bfloat16 [16, 65536], P('orig', 'dest'), may hold values from 0 to 3
- prior: float32 [16, 65536], P('orig', 'dest'), may hold values from -8 to 420
- flows: int32 [16, 65536], P('orig', 'dest'), may hold values from 0 to 4
- w_in: bfloat16 [39, 256], replicated, may hold values from -1 to 1
- w_mid: bfloat16 [2, 256, 256], replicated, may hold values from -0.375 to 0.375
- w_out: bfloat16 [256], replicated, may hold values from -0.375 to 0.375
- biases: bfloat16 [3, 256], replicated, may hold values from -3 to 3
Outputs:
- zone_grad: float32 [19, 65536], P(None, 'dest')
- w_in_grad: float32 [39, 256], replicated
- w_mid_grad: float32 [2, 256, 256], replicated
- w_out_grad: float32 [256], replicated
- bias_grad: float32 [3, 256], replicated
The draws below stay inside these ranges and needn't reach their ends.
All inputs are finite; a program needn't handle non-finite values.
Results may differ from the reference program's by a relative error of at most 0.028.
Values sent between devices are 32-bit elements; how exact they have to be, the bound alone decides.
A program may use at most 64 MiB of HBM per device.

```python
import jax
import jax.numpy as jnp
from jax import lax

H = 256
FZ = 19
ANCHORS = 16
ZONES = 65536
F = 39


def draw_prior(key, part):
    key = jax.random.fold_in(key, 7)
    key_one = jax.random.fold_in(key, 0)
    ramp = 1.1 * jnp.arange(ZONES, dtype=jnp.float32)[None, :] / ZONES
    base = 2.0 * jnp.clip(jax.random.normal(key_one, (ANCHORS, ZONES), jnp.float32), -3.5, 3.5)
    return base + ramp


def draw_flows(key, part):
    key = jax.random.fold_in(key, 11)
    column = jnp.arange(ZONES, dtype=jnp.int32)[None, :]
    upper = 2 + 4 * column // ZONES
    upper = jnp.broadcast_to(upper, (ANCHORS, ZONES))
    return jax.random.randint(key, (ANCHORS, ZONES), 0, upper).astype(jnp.int32)


def with_ends(entries, own_key, smallest, high):
    shape = entries.shape
    spot = [jax.random.randint(jax.random.fold_in(own_key, axis), (), 0, shape[axis]) for axis in range(len(shape))]
    entries = entries.at[tuple(spot)].set(smallest)
    longest = shape.index(max(shape))
    spot[longest] = (spot[longest] + 1) % shape[longest]
    return entries.at[tuple(spot)].set(high)


def levels(rng, extent, cuts, smallest, top_value):
    def one(position, shards_of):
        steps = jax.random.uniform(jax.random.fold_in(jax.random.fold_in(rng, 6), position), (shards_of,), jnp.float32, smallest / len(cuts), top_value / len(cuts))
        return jnp.repeat(jnp.exp(steps), extent[position] // shards_of).reshape((-1,) + (1,) * (len(extent) - position - 1))

    level = one(*cuts[0])
    for cut in cuts[1:]:
        level = level * one(*cut)
    return level


def centred(stream_key, extent, deviation, most, pieces=(), held_as=jnp.bfloat16):
    array = deviation * jax.random.normal(stream_key, extent, jnp.float32)
    if pieces:
        array = array * levels(stream_key, extent, pieces, -0.22, 0.18)
    return jnp.clip(array, -most, most).astype(held_as)


def setup_inputs(seed: int = 0) -> dict:
    splits = jax.random.split(jax.random.key(seed), 10)
    zone_feat = centred(splits[0], (FZ, ZONES), 1.0, 6.0, ((1, 128),))
    anchor_zone = with_ends(jax.random.randint(splits[1], (ANCHORS,), 0, ZONES), jax.random.fold_in(splits[1], 1), 0, ZONES - 1).astype(jnp.int32)
    distance = jnp.clip(3.0 * jax.random.uniform(splits[2], (ANCHORS, ZONES), jnp.float32) ** levels(splits[2], (ANCHORS, ZONES), ((0, 4), (1, 128)), -0.2, 0.2), 0.0, 3.0).astype(jnp.bfloat16)
    prior = draw_prior(jax.random.fold_in(splits[9], 71), 0)
    flows = draw_flows(jax.random.fold_in(splits[9], 71), 0)
    w_in = centred(splits[5], (F, H), F ** -0.5, 1.0)
    w_mid = centred(splits[6], (2, H, H), H ** -0.5, 0.375)
    w_out = centred(splits[7], (H,), H ** -0.5, 0.375)
    biases = centred(splits[8], (3, H), 0.5, 3.0)
    return dict(zone_feat=zone_feat, anchor_zone=anchor_zone, distance=distance, prior=prior, flows=flows, w_in=w_in, w_mid=w_mid, w_out=w_out, biases=biases)


def silu_slope(pre):
    sig = jax.nn.sigmoid(pre)
    return sig + pre * sig * (1.0 - sig)


def forward(anchor_row, zone_feat, distance_row, prior_row, w_in, w_mid, w_out, biases):
    dest_rows = zone_feat.T
    orig_rows = jnp.broadcast_to(anchor_row[None, :], (ZONES, FZ))
    pair_x = jnp.concatenate([orig_rows, dest_rows, distance_row[:, None]], axis=1)
    pre_one = jnp.dot(pair_x, w_in, preferred_element_type=jnp.float32) + biases[0].astype(jnp.float32)
    layer_one = jax.nn.silu(pre_one).astype(jnp.bfloat16)
    pre_two = jnp.dot(layer_one, w_mid[0], preferred_element_type=jnp.float32) + biases[1].astype(jnp.float32)
    layer_two = jax.nn.silu(pre_two).astype(jnp.bfloat16)
    pre_three = jnp.dot(layer_two, w_mid[1], preferred_element_type=jnp.float32) + biases[2].astype(jnp.float32)
    layer_three = jax.nn.silu(pre_three).astype(jnp.bfloat16)
    scores = jnp.dot(layer_three, w_out, preferred_element_type=jnp.float32) + prior_row
    return pair_x, pre_one, pre_two, pre_three, layer_one, layer_two, layer_three, scores


def reference(zone_feat, anchor_zone, distance, prior, flows, w_in, w_mid, w_out, biases):
    zone_index = anchor_zone.astype(jnp.int32)
    anchor_feat = zone_feat[:, zone_index].T

    def score_row(items):
        anchor_row, distance_row, prior_row = items
        return forward(anchor_row, zone_feat, distance_row, prior_row, w_in, w_mid, w_out, biases)[7]

    scores = lax.map(score_row, (anchor_feat, distance, prior))
    top_score = jnp.max(scores, axis=1, keepdims=True)
    exp_total = jnp.sum(jnp.exp(scores - top_score), axis=1, keepdims=True)
    observed = flows.astype(jnp.float32)
    outflow = jnp.sum(observed, axis=1, keepdims=True)
    share = jnp.exp(scores - top_score) / exp_total
    anchor_total_count = jnp.float32(ANCHORS)
    slope = ((outflow * share - observed) / anchor_total_count).astype(jnp.bfloat16)

    def backward(carry, items):
        acc_in, acc_mid, acc_out, acc_bias, acc_zone = carry
        anchor_row, distance_row, prior_row, slope_row = items
        pair_x, pre_one, pre_two, pre_three, layer_one, layer_two, layer_three, unused = forward(anchor_row, zone_feat, distance_row, prior_row, w_in, w_mid, w_out, biases)
        acc_out = acc_out + jnp.dot(slope_row, layer_three, preferred_element_type=jnp.float32)
        delta_three = (slope_row.astype(jnp.float32)[:, None] * w_out.astype(jnp.float32)[None, :] * silu_slope(pre_three)).astype(jnp.bfloat16)
        delta_two = (jnp.dot(delta_three, w_mid[1].T, preferred_element_type=jnp.float32) * silu_slope(pre_two)).astype(jnp.bfloat16)
        delta_one = (jnp.dot(delta_two, w_mid[0].T, preferred_element_type=jnp.float32) * silu_slope(pre_one)).astype(jnp.bfloat16)
        grad_two = jnp.dot(layer_one.T, delta_two, preferred_element_type=jnp.float32)
        grad_three = jnp.dot(layer_two.T, delta_three, preferred_element_type=jnp.float32)
        acc_mid = acc_mid + jnp.stack([grad_two, grad_three])
        acc_in = acc_in + jnp.dot(pair_x.T, delta_one, preferred_element_type=jnp.float32)
        bias_rows = jnp.stack([jnp.sum(delta_one.astype(jnp.float32), 0), jnp.sum(delta_two.astype(jnp.float32), 0), jnp.sum(delta_three.astype(jnp.float32), 0)])
        acc_bias = acc_bias + bias_rows
        acc_zone = acc_zone + jnp.dot(w_in[FZ:2 * FZ], delta_one.T, preferred_element_type=jnp.float32)
        anchor_term = jnp.sum(jnp.dot(delta_one, w_in[:FZ].T, preferred_element_type=jnp.float32), axis=0)
        return (acc_in, acc_mid, acc_out, acc_bias, acc_zone), anchor_term

    start = (jnp.zeros((F, H), jnp.float32), jnp.zeros((2, H, H), jnp.float32), jnp.zeros((H,), jnp.float32), jnp.zeros((3, H), jnp.float32), jnp.zeros((FZ, ZONES), jnp.float32))
    carry, anchor_terms = lax.scan(backward, start, (anchor_feat, distance, prior, slope))
    acc_in, acc_mid, acc_out, acc_bias, acc_zone = carry
    zone_grad = acc_zone.at[:, zone_index].add(anchor_terms.T)
    return zone_grad, acc_in, acc_mid, acc_out, acc_bias
```

```python
import jax
import jax.numpy as jnp
from jax import lax
from jax.experimental import pallas as pl
from jax.experimental.pallas import tpu as pltpu
from jax.sharding import PartitionSpec as P

MESH = pl.DeviceIdType.MESH
F32 = jnp.float32
BF16 = jnp.bfloat16
XN, ZN, CN, YN = 4, 16, 2, 4
OA, NZ, H, FZ = 4, 512, 256, 19
PAIRS = OA * NZ


def nn(a, b):
    return lax.dot_general(a, b, (((1,), (0,)), ((), ())), preferred_element_type=F32)


def nt(a, b):
    return lax.dot_general(a, b, (((1,), (1,)), ((), ())), preferred_element_type=F32)


def tn(a, b):
    return lax.dot_general(a, b, (((0,), (0,)), ((), ())), preferred_element_type=F32)


def iota(shape, dim):
    return lax.broadcasted_iota(jnp.int32, shape, dim)


def total_wait(ref, sem):
    pltpu.make_async_copy(ref, ref, sem).wait()


def send(src, dst, ssem, rsem, device):
    return pltpu.make_async_remote_copy(
        src_ref=src, dst_ref=dst, send_sem=ssem, recv_sem=rsem, device_id=device, device_id_type=MESH
    )


def kernel(
    a_hbm, prior_hbm, flows_hbm, b_hbm, wmid_hbm,
    zout_ref, fout_ref,
    aa, prior_v, flows_v, bb, wm,
    wz, w4, wmt, xt, p0, l1, l2, l3, l1t, l2t, g1, g2, g3, d1, d2, d3, scb,
    row1, rowz1, rowx, rowx1, rowc1, row2, rowz2, rowx2, rowc2,
    ga, gb, cra, crb, sa, sb, yra, yrb, xs, xr, zs, zr, fp, full, zpart, zpr, zsum, zfull,
    lsem, ssem, rsem, ysem, csem,
):
    dest = lax.axis_index("dest")
    y = lax.axis_index("orig")
    x = dest // (ZN * CN)
    z = (dest // CN) % ZN
    c = dest % CN
    zblk = (z // 4) * 4
    piece = z % 4

    def dev(x_, z_, c_, y_):
        return ((x_ * ZN + z_) * CN + c_, y_)

    partner = dev(x, z, 1 - c, y)

    def far(k):
        half = (k + 1) // 2
        return (z + 8 + half * (1 - 2 * (k % 2)) + ZN) % ZN

    barrier = pltpu.get_barrier_semaphore()

    def greet(device):
        pl.semaphore_signal(barrier, inc=1, device_id=device, device_id_type=MESH)

    def greet_far(k, carry):
        greet(dev(x, far(k), c, y))
        return carry

    lax.fori_loop(0, ZN - 1, greet_far, 0)
    for i in range(1, XN):
        greet(dev((x + i) % XN, z, c, y))
    for j in range(1, YN):
        greet(dev(x, z, c, (y + j) % YN))
    greet(partner)

    loads = [
        pltpu.make_async_copy(src, dst, lsem.at[k])
        for k, (src, dst) in enumerate(
            ((a_hbm, aa), (b_hbm, bb), (flows_hbm, flows_v), (prior_hbm, prior_v), (wmid_hbm, wm))
        )
    ]
    for cp in loads:
        cp.start()
    for cp in loads:
        cp.wait()

    zf32 = jnp.concatenate([aa[0:FZ], jnp.zeros((32 - FZ, NZ), F32)], axis=0)
    dist = aa[FZ : FZ + OA]
    ids = aa[24:32]
    worig = jnp.concatenate([bb[0:FZ], jnp.zeros((32 - FZ, H), F32)], axis=0).astype(BF16)
    wz[...] = jnp.concatenate(
        [bb[FZ : 2 * FZ + 1], bb[39:40], jnp.zeros((32 - FZ - 2, H), F32)], axis=0
    ).astype(BF16)
    w4[...] = jnp.concatenate([worig] * OA, axis=0)
    for k in range(2):
        wmt[k] = wm[k].T
    sub32 = iota((32, NZ), 0)
    for o in range(OA):
        rows = jnp.where(sub32 == FZ, dist[o : o + 1], zf32)
        rows = jnp.where((sub32 == FZ + 1) | (sub32 == 24 + o), 1.0, rows)
        xt[0:32, o * NZ : (o + 1) * NZ] = rows.astype(BF16)
    extra = jnp.where(iota((16, PAIRS), 0) == 0, 1.0, 0.0).astype(BF16)
    l1t[H:, :] = extra
    l2t[H:, :] = extra
    zone_ids = (iota((8, NZ), 1) + dest * NZ).astype(F32)
    sub8 = iota((8, NZ), 0)
    own = jnp.where(sub8 < OA, (ids == zone_ids).astype(F32), 0.0).astype(BF16)
    zf4 = jnp.concatenate([zf32.astype(BF16)] * OA, axis=0)
    lane8 = iota((8, 128), 1)
    row8 = iota((8, 128), 0)
    mine = lane8 // 32 == row8
    chosen = nt(own, zf4)
    observed = flows_v[...].astype(F32)
    outflow_here = jnp.sum(observed, axis=1, keepdims=True)
    outflow8 = jnp.concatenate([outflow_here, jnp.zeros((4, 1), F32)], axis=0)
    packed = jnp.where(mine, jnp.where(lane8 % 32 == 31, outflow8, chosen), 0.0)
    row1[...] = jnp.sum(packed, axis=0, keepdims=True)
    for o in range(OA):
        p0[o] = tn(xt[0:32, o * NZ : (o + 1) * NZ], wz[...])

    pl.semaphore_wait(barrier, ZN - 1 + XN - 1 + YN - 1 + 1)

    def z_start(row, got, s):
        def one(k, carry):
            send(row, got.at[z], ssem.at[s], rsem.at[s], dev(x, far(k), c, y)).start()
            return carry

        lax.fori_loop(0, ZN - 1, one, 0)
        got[z] = row[...]

    def x_stage(row, got, s):
        for i in (2, 1, 3):
            send(row, got.at[x], ssem.at[s], rsem.at[s], dev((x + i) % XN, z, c, y)).start()
        got[x] = row[...]
        total_wait(got.at[pl.ds(0, XN - 1)], rsem.at[s])

    def core_stage(row, got, s):
        got[0] = jnp.broadcast_to(row, (8, 128))
        send(got.at[0], got.at[1], ssem.at[s], rsem.at[s], partner).start()
        total_wait(got.at[1], rsem.at[s])

    z_start(row1, rowz1, 0)
    total_wait(rowz1.at[pl.ds(0, ZN - 1)], rsem.at[0])
    rowx[0] = jnp.sum(rowz1[...], axis=0)
    x_stage(rowx.at[0], rowx1, 1)
    core_stage(jnp.sum(rowx1[...], axis=0), rowc1, 2)
    featrow = rowc1[0] + rowc1[1]
    keep = mine & (lane8 % 32 < FZ)
    cvec = nn(jnp.where(keep, featrow, 0.0).astype(BF16), w4[...])
    outflow = jnp.sum(jnp.where(mine & (lane8 % 32 == 31), featrow, 0.0), axis=1, keepdims=True)

    b1 = bb[40:41]
    b2 = bb[41:42]
    wout = bb[42:43]
    wout16 = jnp.broadcast_to(wout, (16, H)).astype(BF16)

    def act(v):
        s = 0.5 * jnp.tanh(0.5 * v) + 0.5
        l = v * s
        return l.astype(BF16), s + l - l * s

    for o in range(OA):
        a1, k1 = act(p0[o] + cvec[o : o + 1])
        l1[o] = a1
        g1[o] = k1
        a2, k2 = act(nn(a1, wm[0]) + b1)
        l2[o] = a2
        g2[o] = k2
        a3, k3 = act(nn(a2, wm[1]) + b2)
        l3[o] = a3
        g3[o] = k3
        scb[o] = nt(wout16, a3)

    scores = jnp.zeros((8, NZ), F32)
    for o in range(OA):
        scores = jnp.where(sub8 == o, scb[o, 0:8], scores)
    scores = scores[0:OA] + prior_v[...]
    top = jnp.max(scores, axis=1, keepdims=True)
    part = jnp.sum(jnp.exp(scores - top), axis=1, keepdims=True)
    lane4 = iota((OA, 128), 1)
    row4 = iota((OA, 128), 0)
    row2[...] = jnp.sum(
        jnp.where(lane4 == row4, top, 0.0) + jnp.where(lane4 == row4 + 64, part, 0.0), axis=0, keepdims=True
    )
    z_start(row2, rowz2, 3)

    for o in range(OA):
        l1t[0:H, o * NZ : (o + 1) * NZ] = l1[o].T
        l2t[0:H, o * NZ : (o + 1) * NZ] = l2[o].T
    square = (iota((128, 128), 0) == iota((128, 128), 1)) & (iota((128, 128), 1) % 32 < FZ)
    spread = nn(jnp.where(square, featrow[0:1], 0.0).astype(BF16), jnp.ones((128, NZ), BF16)).astype(BF16)
    for o in range(OA):
        xt[32:64, o * NZ : (o + 1) * NZ] = spread[o * 32 : (o + 1) * 32]

    def merge(stats):
        lane = iota((1, 128), 1)
        moved = pltpu.roll(stats, 64, 1)
        big = jnp.max(stats, axis=0, keepdims=True)
        high = jnp.max(moved, axis=0, keepdims=True)
        factor = jnp.exp(jnp.where(lane >= 64, moved - high, 0.0))
        return jnp.where(lane < 64, big, jnp.sum(stats * factor, axis=0, keepdims=True))

    total_wait(rowz2.at[pl.ds(0, ZN - 1)], rsem.at[3])
    rowx[1] = merge(rowz2[:, 0, :])
    x_stage(rowx.at[1], rowx2, 4)
    core_stage(merge(rowx2[:, 0, :]), rowc2, 5)
    pair = jnp.where(row8 == 0, rowc2[0], rowc2[1])
    total = jnp.broadcast_to(merge(pair[0:2]), (OA, 128))
    top_all = jnp.sum(jnp.where(lane4 == row4, total, 0.0), axis=1, keepdims=True)
    sum_all = jnp.sum(jnp.where(lane4 == row4 + 64, total, 0.0), axis=1, keepdims=True)
    share = jnp.exp(scores - top_all) / sum_all
    slope = (outflow[0:OA] * share - observed) * (1.0 / 16.0)
    slope16 = jnp.concatenate([slope, jnp.zeros((12, NZ), F32)], axis=0).astype(BF16)

    sub16 = iota((16, H), 0)
    for o in range(OA):
        u = tn(slope16, jnp.where(sub16 == o, wout, 0.0).astype(BF16))
        d3[o * NZ : (o + 1) * NZ, :] = (u * g3[o]).astype(BF16)
    grad_three = nn(l2t[...], d3[...])
    for h in range(2):
        ga[h] = grad_three[0:H, h * 128 : (h + 1) * 128]

    def core_start(src, dst, s):
        n = dst.shape[0] // 4
        for k in range(4):
            span = pl.ds(k * n, n)
            send(src.at[1 - c, span], dst.at[span], ssem.at[s], rsem.at[s], partner).start()

    def y_start(src, dst, s):
        for j in range(1, YN):
            yt_ = (y + j) % YN
            send(src.at[yt_], dst.at[y], ssem.at[s], rsem.at[s], dev(x, z, c, yt_)).start()
        dst[y] = src[y]

    three = pl.ds(0, 3)
    core_start(ga, cra, 6)
    for o in range(OA):
        span = slice(o * NZ, (o + 1) * NZ)
        d2[span, :] = (nn(d3[span, :], wmt[1]) * g2[o]).astype(BF16)
    grad_two = nn(l1t[...], d2[...])
    for h in range(2):
        gb[h, 0:H] = grad_two[0:H, h * 128 : (h + 1) * 128]
    total_wait(cra, rsem.at[6])
    sa[...] = (ga[c] + cra[...]).reshape(4, 64, 128)
    y_start(sa, yra, 7)

    zone = jnp.zeros((32, NZ), F32)
    for o in range(OA):
        span = slice(o * NZ, (o + 1) * NZ)
        d1o = (nn(d2[span, :], wmt[0]) * g1[o]).astype(BF16)
        d1[span, :] = d1o
        zone = zone + nt(wz[...], d1o)
    grad_in = nn(xt[...], d1[...])
    gout = jnp.zeros((16, H), F32)
    for o in range(OA):
        gout = gout + jnp.where(sub16 == o, nn(slope16, l3[o]), 0.0)
    gout = jnp.sum(gout, axis=0, keepdims=True)
    per_anchor = grad_in[24:32]
    high = per_anchor.astype(BF16)
    mid = (per_anchor - high.astype(F32)).astype(BF16)
    term = jnp.where(mine, nt(high, w4[...]) + nt(mid, w4[...]), 0.0)
    tag = jnp.where(mine & (lane8 % 32 == 20) & (dest == 0), ids[:, 0:128], 0.0)
    term = jnp.sum(term + tag, axis=0, keepdims=True)
    row8h = iota((8, H), 0)
    mixed = jnp.where(row8h == 0, grad_two[H : H + 1], 0.0)
    mixed = jnp.where(row8h == 1, grad_three[H : H + 1], mixed)
    mixed = jnp.where(row8h == 2, gout, mixed)
    for h in range(2):
        span = slice(h * 128, (h + 1) * 128)
        gb[h, H : H + 24] = grad_in[0:24, span]
        tile = mixed[:, span]
        if h == 0:
            tile = jnp.where(row8 == 4 + y, term, tile)
        gb[h, H + 24 : H + 32] = tile
        gb[h, H + 32 : H + 64] = grad_in[32:64, span]
    core_start(gb, crb, 8)
    for j in range(YN):
        zpart[j] = zone[0:24, j * 128 : (j + 1) * 128]
    y_start(zpart, zpr, 9)
    total_wait(crb, rsem.at[8])
    both = gb[c] + crb[...]
    sb[:, 0:64] = both[0:H].reshape(4, 64, 128)
    sb[:, 64:80] = both[H:].reshape(4, 16, 128)
    y_start(sb, yrb, 10)

    total_wait(yra.at[three], rsem.at[7])
    xs[:, 0:16] = jnp.sum(yra[...], axis=0).reshape(4, 16, 128)
    total_wait(zpr.at[three], rsem.at[9])
    zsum[...] = jnp.sum(zpr[...], axis=0)
    for j in range(1, YN):
        send(zsum, zfull.at[y], ssem.at[11], rsem.at[11], dev(x, z, c, (y + j) % YN)).start()
    zfull[y] = zsum[...]
    total_wait(yrb.at[three], rsem.at[10])
    sum_b = jnp.sum(yrb[...], axis=0)
    xs[:, 16:32] = sum_b[0:64].reshape(4, 16, 128)
    xs[:, 32:36] = sum_b[64:80].reshape(4, 4, 128)
    for i in range(1, XN):
        xt_ = (x + i) % XN
        send(xs.at[xt_], xr.at[x], ssem.at[12], rsem.at[12], dev(xt_, z, c, y)).start()
    xr[x] = xs[x]
    total_wait(xr.at[three], rsem.at[12])
    sum_x = jnp.sum(xr[...], axis=0)
    for p in range(4):
        zs[p, 0:8] = sum_x[p * 8 : (p + 1) * 8]
        zs[p, 8:9] = sum_x[32 + p : 33 + p]

    def z_one(k, carry):
        zt = far(k)
        send(zs.at[zt % 4], zr.at[z], ssem.at[13], rsem.at[13], dev(x, zt, c, y)).start()
        return carry

    lax.fori_loop(0, ZN - 1, z_one, 0)
    zr[z] = zs[piece]
    total_wait(zr.at[pl.ds(0, ZN - 1)], rsem.at[13])
    fp[...] = jnp.sum(zr[...], axis=0)

    for k in range(1, 4):
        send(fp, full.at[c, y, x, piece], ssem.at[14], rsem.at[14], dev(x, zblk + (z + k) % 4, c, y)).start()
    full[c, y, x, piece] = fp[...]
    total_wait(full.at[c, y, x, three], rsem.at[14])
    for i in range(1, XN):
        send(full.at[c, y, x], full.at[c, y, x], ssem.at[15], rsem.at[15], dev((x + i) % XN, z, c, y)).start()
    total_wait(full.at[c, y, three], rsem.at[15])
    for j in range(1, YN):
        send(full.at[c, y], full.at[c, y], ssem.at[16], ysem.at[j - 1], dev(x, z, c, (y + j) % YN)).start()
    send(full.at[c, y], full.at[c, y], ssem.at[17], csem.at[0], partner).start()
    for j in range(1, YN):
        yf = (y - j + YN) % YN
        total_wait(full.at[c, yf], ysem.at[j - 1])
        send(full.at[c, yf], full.at[c, yf], ssem.at[17], csem.at[j], partner).start()
    total_wait(zfull.at[three], rsem.at[11])
    for j in range(YN):
        zout_ref[:, j * 128 : (j + 1) * 128] = zfull[j]
    for j in range(YN):
        total_wait(full.at[1 - c, (y - j + YN) % YN], csem.at[j])
    fout_ref[...] = full[...]

    for s, ref in (
        (0, rowz1.at[pl.ds(0, ZN - 1)]), (1, rowx1.at[three]), (2, rowc1.at[1]),
        (3, rowz2.at[pl.ds(0, ZN - 1)]), (4, rowx2.at[three]), (5, rowc2.at[1]),
        (6, cra), (7, yra.at[three]), (8, crb), (9, zpr.at[three]), (10, yrb.at[three]), (11, zfull.at[three]),
        (12, xr.at[three]), (13, zr.at[pl.ds(0, ZN - 1)]), (14, full.at[c, y, x, three]),
        (15, full.at[c, y, three]), (16, full.at[c, three]), (17, full.at[c]),
    ):
        total_wait(ref, ssem.at[s])


def finish(f_ref, zone_ref, zg_ref, gin_ref, gmid_ref, gout_ref, gbias_ref):
    dest = lax.axis_index("dest")
    for h in range(2):
        span = slice(h * 128, (h + 1) * 128)
        for q in range(16):
            for p in range(4):
                r = q * 16 + (p % 2) * 8
                gmid_ref[1 - p // 2, r : r + 8, span] = f_ref[h, q // 4, q % 4, p, 0:8]
        small = f_ref[h, :, :, :, 8, :].reshape(64, 128)
        gin_ref[0:FZ, span] = small[32 : 32 + FZ]
        gin_ref[FZ : 2 * FZ + 1, span] = small[0 : FZ + 1]
        gbias_ref[0:1, span] = small[20:21]
        gbias_ref[1:3, span] = small[24:26]
        gout_ref[0:1, span] = small[26:27]
        if h == 0:
            atm = small[28:32]
    table = jnp.concatenate(
        [jnp.concatenate([atm[:, o * 32 : (o + 1) * 32], jnp.zeros((4, 32), F32)], axis=0) for o in range(OA)],
        axis=0,
    )
    hits = (table[:, 20:21] == (iota((32, NZ), 1) + dest * NZ).astype(F32)).astype(F32)
    added = lax.dot_general(
        table, hits, (((0,), (0,)), ((), ())), preferred_element_type=F32, precision=lax.Precision.HIGHEST
    )
    zg_ref[...] = zone_ref[0:FZ] + added[0:FZ]


def per_device(zone_feat, anchor_zone, distance, prior, flows, w_in, w_mid, w_out, biases):
    vm = pltpu.VMEM
    dma = pltpu.SemaphoreType.DMA
    ids = jnp.broadcast_to(anchor_zone.astype(F32)[:, None], (OA, NZ))
    a = jnp.concatenate(
        [zone_feat.astype(F32), distance.astype(F32), jnp.zeros((1, NZ), F32), ids, jnp.zeros((4, NZ), F32)], axis=0
    )
    b = jnp.concatenate(
        [w_in.astype(F32), biases.astype(F32), w_out.astype(F32)[None, :], jnp.zeros((5, H), F32)], axis=0
    )
    shapes = [
        vm((32, NZ), F32), vm((OA, NZ), F32), vm((OA, NZ), jnp.int32), vm((48, H), F32), vm((2, H, H), BF16),
        vm((32, H), BF16), vm((128, H), BF16), vm((2, H, H), BF16), vm((64, PAIRS), BF16),
        vm((OA, NZ, H), F32), vm((OA, NZ, H), BF16), vm((OA, NZ, H), BF16), vm((OA, NZ, H), BF16),
        vm((H + 16, PAIRS), BF16), vm((H + 16, PAIRS), BF16),
        vm((OA, NZ, H), F32), vm((OA, NZ, H), F32), vm((OA, NZ, H), F32),
        vm((PAIRS, H), BF16), vm((PAIRS, H), BF16), vm((PAIRS, H), BF16), vm((OA, 16, NZ), F32),
        vm((1, 128), F32), vm((ZN, 1, 128), F32), vm((2, 1, 128), F32), vm((XN, 1, 128), F32), vm((2, 8, 128), F32),
        vm((1, 128), F32), vm((ZN, 1, 128), F32), vm((XN, 1, 128), F32), vm((2, 8, 128), F32),
        vm((2, H, 128), F32), vm((2, H + 64, 128), F32), vm((H, 128), F32), vm((H + 64, 128), F32),
        vm((4, 64, 128), F32), vm((4, 80, 128), F32), vm((4, 64, 128), F32), vm((4, 80, 128), F32),
        vm((4, 36, 128), F32), vm((4, 36, 128), F32),
        vm((4, 9, 128), F32), vm((ZN, 9, 128), F32), vm((9, 128), F32), vm((2, YN, XN, 4, 9, 128), F32),
        vm((YN, 24, 128), F32), vm((YN, 24, 128), F32), vm((24, 128), F32), vm((YN, 24, 128), F32),
        dma((5,)), dma((18,)), dma((18,)), dma((3,)), dma((4,)),
    ]
    vspec = pl.BlockSpec(memory_space=pltpu.VMEM)
    anyspec = pl.BlockSpec(memory_space=pl.ANY)
    zone, parts = pl.pallas_call(
        kernel,
        out_shape=(
            jax.ShapeDtypeStruct((24, NZ), F32),
            jax.ShapeDtypeStruct((2, YN, XN, 4, 9, 128), F32),
        ),
        in_specs=[anyspec] * 5,
        out_specs=[vspec] * 2,
        scratch_shapes=shapes,
        compiler_params=pltpu.CompilerParams(
            collective_id=0, has_side_effects=True, vmem_limit_bytes=48 * 2**20
        ),
        name="gravity_backward",
    )(a, prior, flows, b, w_mid)
    out = pl.pallas_call(
        finish,
        out_shape=(
            jax.ShapeDtypeStruct((FZ, NZ), F32),
            jax.ShapeDtypeStruct((2 * FZ + 1, H), F32),
            jax.ShapeDtypeStruct((2, H, H), F32),
            jax.ShapeDtypeStruct((1, H), F32),
            jax.ShapeDtypeStruct((3, H), F32),
        ),
        in_specs=[vspec] * 2,
        out_specs=[vspec] * 5,
        name="results",
    )(parts, zone)
    return out[0], out[1], out[2], out[3].reshape(H), out[4]


def solution(mesh):
    in_specs = (
        P(None, "dest"), P("orig"), P("orig", "dest"), P("orig", "dest"), P("orig", "dest"), P(), P(), P(), P(),
    )
    out_specs = (P(None, "dest"), P(), P(), P(), P())
    return jax.shard_map(
        per_device, mesh=mesh, in_specs=in_specs, out_specs=out_specs, check_vma=False
    )
```

```python
import jax
import jax.numpy as jnp
from jax import lax
from jax.experimental import pallas as pl
from jax.experimental.pallas import tpu as pltpu
from jax.sharding import PartitionSpec as P

MESH = pl.DeviceIdType.MESH
F32 = jnp.float32
BF16 = jnp.bfloat16
XN, ZN, CN, YN = 4, 16, 2, 4
OA, NZ, H, FZ = 4, 512, 256, 19
PAIRS = OA * NZ
FAR = (8, 7, 9, 6, 10, 5, 11, 4, 12, 3, 13, 2, 14, 1, 15)


def nn(a, b):
    return lax.dot_general(a, b, (((1,), (0,)), ((), ())), preferred_element_type=F32)


def nt(a, b):
    return lax.dot_general(a, b, (((1,), (1,)), ((), ())), preferred_element_type=F32)


def tn(a, b):
    return lax.dot_general(a, b, (((0,), (0,)), ((), ())), preferred_element_type=F32)


def iota(shape, dim):
    return lax.broadcasted_iota(jnp.int32, shape, dim)


def total_wait(ref, sem):
    pltpu.make_async_copy(ref, ref, sem).wait()


def send(src, dst, ssem, rsem, device):
    return pltpu.make_async_remote_copy(
        src_ref=src, dst_ref=dst, send_sem=ssem, recv_sem=rsem, device_id=device, device_id_type=MESH
    )


def kernel(
    a_hbm, az_hbm, prior_hbm, flows_hbm, wmid_hbm,
    zout_ref, fout_ref,
    ab, az, prior_v, flows_v, wm,
    wz, w4, wmt, xt, p0, l1, l2, l3, l1t, l2t, g1, g2, g3, d1, d2, d3, scb,
    row1, rowz1, rowx, rowx1, rowc1, row2, rowz2, rowx2, rowc2,
    ga, gb, cra, crb, sa, sb, yra, yrb, zs, zr, fp, full, zpart, zpr, zsum, zfull,
    lsem, ssem, rsem, ysem, csem, osem,
):
    dest = lax.axis_index("dest")
    y = lax.axis_index("orig")
    x = dest // (ZN * CN)
    z = (dest // CN) % ZN
    c = dest % CN
    zblk = (z // 4) * 4
    piece = z % 4
    me_q = y * XN + x

    def dev(x_, z_, c_, y_):
        return ((x_ * ZN + z_) * CN + c_, y_)

    partner = dev(x, z, 1 - c, y)

    barrier = pltpu.get_barrier_semaphore()

    def greet(device):
        pl.semaphore_signal(barrier, inc=1, device_id=device, device_id_type=MESH)

    for t in FAR:
        greet(dev(x, (z + t) % ZN, c, y))
    for k in range(1, XN * YN):
        greet(dev((x + k // YN) % XN, z, c, (y + k) % YN))
    greet(partner)

    loads = [
        pltpu.make_async_copy(src, dst, lsem.at[k])
        for k, (src, dst) in enumerate(
            ((a_hbm, ab), (az_hbm, az), (flows_hbm, flows_v), (prior_hbm, prior_v), (wmid_hbm, wm))
        )
    ]
    for cp in loads:
        cp.start()
    for cp in loads:
        cp.wait()

    zfd = ab[0:32].astype(F32)
    dist = zfd[24 : 24 + OA]
    zf32 = jnp.where(iota((32, NZ), 0) < FZ, zfd, 0.0)
    bb = ab[32:80, 0:H].astype(F32)
    worig = jnp.where(iota((32, H), 0) < FZ, bb[0:32], 0.0).astype(BF16)
    wz[...] = jnp.concatenate(
        [bb[FZ : 2 * FZ + 1], bb[40:41], jnp.zeros((32 - FZ - 2, H), F32)], axis=0
    ).astype(BF16)
    w4[...] = jnp.concatenate([worig] * OA, axis=0)
    for k in range(2):
        wmt[k] = wm[k].T
    sub32 = iota((32, NZ), 0)
    for o in range(OA):
        rows = jnp.where(sub32 == FZ, dist[o : o + 1], zf32)
        rows = jnp.where((sub32 == FZ + 1) | (sub32 == 24 + o), 1.0, rows)
        xt[0:32, o * NZ : (o + 1) * NZ] = rows.astype(BF16)
    extra = jnp.where(iota((16, PAIRS), 0) == 0, 1.0, 0.0).astype(BF16)
    l1t[H:, :] = extra
    l2t[H:, :] = extra
    zone_ids = iota((8, NZ), 1) + dest * NZ
    sub8 = iota((8, NZ), 0)
    ids = jnp.full((8, NZ), -1, jnp.int32)
    for o in range(OA):
        ids = jnp.where(sub8 == o, az[o], ids)
    own = (ids == zone_ids).astype(F32).astype(BF16)
    zf4 = jnp.concatenate([zf32.astype(BF16)] * OA, axis=0)
    lane8 = iota((8, 128), 1)
    row8 = iota((8, 128), 0)
    mine = lane8 // 32 == row8
    chosen = nt(own, zf4)
    observed = flows_v[...].astype(F32)
    outflow_here = jnp.sum(observed, axis=1, keepdims=True)
    outflow8 = jnp.concatenate([outflow_here, jnp.zeros((4, 1), F32)], axis=0)
    packed = jnp.where(mine, jnp.where(lane8 % 32 == 31, outflow8, chosen), 0.0)
    row1[...] = jnp.sum(packed, axis=0, keepdims=True)
    for o in range(OA):
        p0[o] = tn(xt[0:32, o * NZ : (o + 1) * NZ], wz[...])

    pl.semaphore_wait(barrier, ZN - 1 + XN * YN - 1 + 1)

    def z_start(row, got, s):
        for t in FAR:
            send(row, got.at[z], ssem.at[s], rsem.at[s], dev(x, (z + t) % ZN, c, y)).start()
        got[z] = row[...]

    def x_stage(row, got, s):
        for i in (2, 1, 3):
            send(row, got.at[x], ssem.at[s], rsem.at[s], dev((x + i) % XN, z, c, y)).start()
        got[x] = row[...]
        total_wait(got.at[pl.ds(0, XN - 1)], rsem.at[s])

    def core_stage(row, got, s):
        got[0] = jnp.broadcast_to(row, (8, 128))
        send(got.at[0], got.at[1], ssem.at[s], rsem.at[s], partner).start()
        total_wait(got.at[1], rsem.at[s])

    z_start(row1, rowz1, 0)
    total_wait(rowz1.at[pl.ds(0, ZN - 1)], rsem.at[0])
    rowx[0] = jnp.sum(rowz1[...], axis=0)
    x_stage(rowx.at[0], rowx1, 1)
    core_stage(jnp.sum(rowx1[...], axis=0), rowc1, 2)
    featrow = rowc1[0] + rowc1[1]
    keep = mine & (lane8 % 32 < FZ)
    cvec = nn(jnp.where(keep, featrow, 0.0).astype(BF16), w4[...])
    outflow = jnp.sum(jnp.where(mine & (lane8 % 32 == 31), featrow, 0.0), axis=1, keepdims=True)

    b1 = bb[41:42]
    b2 = bb[42:43]
    wout = bb[47:48]
    wout16 = jnp.broadcast_to(wout, (16, H)).astype(BF16)

    def act(v):
        s = 0.5 * jnp.tanh(0.5 * v) + 0.5
        l = v * s
        return l.astype(BF16), s + l - l * s

    for o in range(OA):
        a1, k1 = act(p0[o] + cvec[o : o + 1])
        l1[o] = a1
        g1[o] = k1
        a2, k2 = act(nn(a1, wm[0]) + b1)
        l2[o] = a2
        g2[o] = k2
        a3, k3 = act(nn(a2, wm[1]) + b2)
        l3[o] = a3
        g3[o] = k3 * wout
        scb[o] = nt(wout16, a3)

    scores = jnp.zeros((8, NZ), F32)
    for o in range(OA):
        scores = jnp.where(sub8 == o, scb[o, 0:8], scores)
    scores = scores[0:OA] + prior_v[...]
    top = jnp.max(scores, axis=1, keepdims=True)
    part = jnp.sum(jnp.exp(scores - top), axis=1, keepdims=True)
    lane4 = iota((OA, 128), 1)
    row4 = iota((OA, 128), 0)
    row2[...] = jnp.sum(
        jnp.where(lane4 == row4, top, 0.0) + jnp.where(lane4 == row4 + 64, part, 0.0), axis=0, keepdims=True
    )
    z_start(row2, rowz2, 3)

    for o in range(OA):
        l1t[0:H, o * NZ : (o + 1) * NZ] = l1[o].T
        l2t[0:H, o * NZ : (o + 1) * NZ] = l2[o].T
    square = (iota((128, 128), 0) == iota((128, 128), 1)) & (iota((128, 128), 1) % 32 < FZ)
    spread = nn(jnp.where(square, featrow[0:1], 0.0).astype(BF16), jnp.ones((128, NZ), BF16)).astype(BF16)
    for o in range(OA):
        xt[32:64, o * NZ : (o + 1) * NZ] = spread[o * 32 : (o + 1) * 32]

    def merge(stats):
        lane = iota((1, 128), 1)
        moved = pltpu.roll(stats, 64, 1)
        big = jnp.max(stats, axis=0, keepdims=True)
        high = jnp.max(moved, axis=0, keepdims=True)
        factor = jnp.exp(jnp.where(lane >= 64, moved - high, 0.0))
        return jnp.where(lane < 64, big, jnp.sum(stats * factor, axis=0, keepdims=True))

    total_wait(rowz2.at[pl.ds(0, ZN - 1)], rsem.at[3])
    rowx[1] = merge(rowz2[:, 0, :])
    x_stage(rowx.at[1], rowx2, 4)
    core_stage(merge(rowx2[:, 0, :]), rowc2, 5)
    pair = jnp.where(row8 == 0, rowc2[0], rowc2[1])
    total = jnp.broadcast_to(merge(pair[0:2]), (OA, 128))
    top_all = jnp.sum(jnp.where(lane4 == row4, total, 0.0), axis=1, keepdims=True)
    sum_all = jnp.sum(jnp.where(lane4 == row4 + 64, total, 0.0), axis=1, keepdims=True)
    share = jnp.exp(scores - top_all) / sum_all
    slope = (outflow[0:OA] * share - observed) * (1.0 / 16.0)
    slope16 = jnp.concatenate([slope, jnp.zeros((12, NZ), F32)], axis=0).astype(BF16)

    sub16 = iota((16, H), 0)
    gout = jnp.zeros((8, H), F32)
    for o in range(OA):
        u = tn(slope16, jnp.where(sub16 == o, 1.0, 0.0).astype(BF16))
        d3[o * NZ : (o + 1) * NZ, :] = (u * g3[o]).astype(BF16)
        gout = gout + jnp.sum((u * l3[o].astype(F32)).reshape(NZ // 8, 8, H), axis=0)
    grad_three = nn(l2t[...], d3[...])
    for h in range(2):
        ga[h] = grad_three[0:H, h * 128 : (h + 1) * 128]

    def core_start(src, dst, s):
        n = dst.shape[0] // 4
        for k in range(4):
            span = pl.ds(k * n, n)
            send(src.at[1 - c, span], dst.at[span], ssem.at[s], rsem.at[s], partner).start()

    def y_start(src, dst, s):
        for j in range(1, YN):
            yt_ = (y + j) % YN
            send(src.at[yt_], dst.at[y], ssem.at[s], rsem.at[s], dev(x, z, c, yt_)).start()
        dst[y] = src[y]

    def xy_start(src, dst, s):
        for k in range(1, XN * YN):
            xt_, yt_ = (x + k // YN) % XN, (y + k) % YN
            send(src.at[yt_ * XN + xt_], dst.at[me_q], ssem.at[s], rsem.at[s], dev(xt_, z, c, yt_)).start()
        dst[me_q] = src[me_q]

    three = pl.ds(0, 3)
    fifteen = pl.ds(0, 15)
    core_start(ga, cra, 6)
    for o in range(OA):
        span = slice(o * NZ, (o + 1) * NZ)
        d2[span, :] = (nn(d3[span, :], wmt[1]) * g2[o]).astype(BF16)
    grad_two = nn(l1t[...], d2[...])
    for h in range(2):
        gb[h, 0:H] = grad_two[0:H, h * 128 : (h + 1) * 128]
    total_wait(cra, rsem.at[6])
    sa[...] = (ga[c] + cra[...]).reshape(16, 16, 128)
    xy_start(sa, yra, 7)

    for o in range(OA):
        span = slice(o * NZ, (o + 1) * NZ)
        d1[span, :] = (nn(d2[span, :], wmt[0]) * g1[o]).astype(BF16)
    grad_in = nn(xt[...], d1[...])
    gout = jnp.sum(gout, axis=0, keepdims=True)
    per_anchor = grad_in[24:32]
    high = per_anchor.astype(BF16)
    mid = (per_anchor - high.astype(F32)).astype(BF16)
    term = jnp.where(mine, nt(high, w4[...]) + nt(mid, w4[...]), 0.0)
    tag = jnp.where(mine & (lane8 % 32 == 20) & (dest == 0), ids[:, 0:128].astype(F32), 0.0)
    term = jnp.sum(term + tag, axis=0, keepdims=True)
    row8h = iota((8, H), 0)
    mixed = jnp.where(row8h == 0, grad_two[H : H + 1], 0.0)
    mixed = jnp.where(row8h == 1, grad_three[H : H + 1], mixed)
    mixed = jnp.where(row8h == 2, gout, mixed)
    for h in range(2):
        span = slice(h * 128, (h + 1) * 128)
        gb[h, H : H + 24] = grad_in[0:24, span]
        tile = mixed[:, span]
        if h == 0:
            tile = jnp.where(row8 == 4 + y, term, tile)
        gb[h, H + 24 : H + 32] = tile
        gb[h, H + 32 : H + 64] = grad_in[32:64, span]
    core_start(gb, crb, 8)
    zone = jnp.zeros((32, NZ), F32)
    for o in range(OA):
        zone = zone + nt(wz[...], d1[o * NZ : (o + 1) * NZ, :])
    total_wait(crb, rsem.at[8])
    both = gb[c] + crb[...]
    sb[:, 0:16] = both[0:H].reshape(16, 16, 128)
    sb[:, 16:20] = both[H:].reshape(16, 4, 128)
    xy_start(sb, yrb, 10)
    for j in range(YN):
        zpart[j] = zone[0:24, j * 128 : (j + 1) * 128]
    y_start(zpart, zpr, 9)
    total_wait(zpr.at[three], rsem.at[9])
    zsum[...] = jnp.sum(zpr[...], axis=0)
    for j in range(1, YN):
        send(zsum, zfull.at[y], ssem.at[11], rsem.at[11], dev(x, z, c, (y + j) % YN)).start()
    zfull[y] = zsum[...]
    total_wait(yra.at[fifteen], rsem.at[7])
    sum_a = jnp.sum(yra[...], axis=0)
    total_wait(yrb.at[fifteen], rsem.at[10])
    sum_b = jnp.sum(yrb[...], axis=0)
    zs[0, 0:8] = sum_a[0:8]
    zs[1, 0:8] = sum_a[8:16]
    zs[2, 0:8] = sum_b[0:8]
    zs[3, 0:8] = sum_b[8:16]
    for p in range(4):
        zs[p, 8:9] = sum_b[16 + p : 17 + p]

    for t in FAR:
        zt = (z + t) % ZN
        send(zs.at[zt % 4], zr.at[z], ssem.at[13], rsem.at[13], dev(x, zt, c, y)).start()
    zr[z] = zs[piece]
    total_wait(zr.at[pl.ds(0, ZN - 1)], rsem.at[13])
    fp[...] = jnp.sum(zr[...], axis=0)

    for k in range(1, 4):
        send(fp, full.at[c, y, x, piece], ssem.at[14], rsem.at[14], dev(x, zblk + (z + k) % 4, c, y)).start()
    full[c, y, x, piece] = fp[...]
    total_wait(full.at[c, y, x, three], rsem.at[14])
    block = full.at[c, y, x]
    stores = []
    for i in range(1, XN):
        send(block, block, ssem.at[16], ysem.at[0], dev((x + i) % XN, z, c, y)).start()
    for j in range(1, YN):
        for i in range(XN):
            send(block, block, ssem.at[12], ysem.at[j], dev((x + i) % XN, z, c, (y + j) % YN)).start()
    for j in range(YN):
        yf = (y - j + YN) % YN
        rowset = full.at[c, yf]
        total_wait(rowset if j else full.at[c, yf, three], ysem.at[j])
        send(rowset, rowset, ssem.at[15], csem.at[j], partner).start()
        stores.append(pltpu.make_async_copy(rowset, fout_ref.at[c, yf], osem.at[j]))
        stores[-1].start()
    total_wait(zfull.at[three], rsem.at[11])
    stores.append(pltpu.make_async_copy(zfull, zout_ref, osem.at[2 * YN]))
    stores[-1].start()
    for j in range(YN):
        yf = (y - j + YN) % YN
        total_wait(full.at[1 - c, yf], csem.at[j])
        stores.append(pltpu.make_async_copy(full.at[1 - c, yf], fout_ref.at[1 - c, yf], osem.at[YN + j]))
        stores[-1].start()
    for cp in stores:
        cp.wait()

    for s, ref in (
        (0, rowz1.at[pl.ds(0, ZN - 1)]), (1, rowx1.at[three]), (2, rowc1.at[1]),
        (3, rowz2.at[pl.ds(0, ZN - 1)]), (4, rowx2.at[three]), (5, rowc2.at[1]),
        (6, cra), (7, yra.at[fifteen]), (8, crb), (9, zpr.at[three]), (10, yrb.at[fifteen]), (11, zfull.at[three]),
        (12, full.at[c, three]), (16, full.at[c, y, three]), (13, zr.at[pl.ds(0, ZN - 1)]), (14, full.at[c, y, x, three]), (15, full.at[c]),
    ):
        total_wait(ref, ssem.at[s])


def finish(f_any, zone_any, zg_ref, gin_ref, gmid_ref, gout_ref, gbias_ref, f_ref, zone_ref, sem):
    dest = lax.axis_index("dest")
    loads = [pltpu.make_async_copy(f_any, f_ref, sem.at[0]), pltpu.make_async_copy(zone_any, zone_ref, sem.at[1])]
    for cp in loads:
        cp.start()
    for cp in loads:
        cp.wait()
    for h in range(2):
        span = slice(h * 128, (h + 1) * 128)
        for q in range(16):
            for p in range(4):
                r = q * 16 + (p % 2) * 8
                gmid_ref[1 - p // 2, r : r + 8, span] = f_ref[h, q // 4, q % 4, p, 0:8]
        small = f_ref[h, :, :, :, 8, :].reshape(64, 128)
        gin_ref[0:FZ, span] = small[32 : 32 + FZ]
        gin_ref[FZ : 2 * FZ + 1, span] = small[0 : FZ + 1]
        gbias_ref[0:1, span] = small[20:21]
        gbias_ref[1:3, span] = small[24:26]
        gout_ref[0:1, span] = small[26:27]
        if h == 0:
            atm = small[28:32]
    table = jnp.concatenate(
        [jnp.concatenate([atm[:, o * 32 : (o + 1) * 32], jnp.zeros((4, 32), F32)], axis=0) for o in range(OA)],
        axis=0,
    )
    hits = (table[:, 20:21] == (iota((32, NZ), 1) + dest * NZ).astype(F32)).astype(F32)
    added = lax.dot_general(
        table, hits, (((0,), (0,)), ((), ())), preferred_element_type=F32, precision=lax.Precision.HIGHEST
    )
    for j in range(YN):
        span = slice(j * 128, (j + 1) * 128)
        zg_ref[:, span] = zone_ref[j, 0:FZ] + added[0:FZ, span]


def per_device(zone_feat, anchor_zone, distance, prior, flows, w_in, w_mid, w_out, biases):
    vm = pltpu.VMEM
    dma = pltpu.SemaphoreType.DMA
    def place(array, row, lane):
        rows, lanes = array.shape
        return lax.pad(array, BF16(0), ((row, 80 - row - rows, 0), (lane, NZ - lane - lanes, 0)))

    packed = place(zone_feat, 0, 0) + place(distance, 24, 0) + place(w_in, 32, 0) + place(biases, 72, 0)
    last = lax.pad(w_out, BF16(0), ((0, NZ - H, 0),))
    packed = packed + jnp.where(iota((80, NZ), 0) == 79, last[None, :], BF16(0))
    shapes = [
        vm((80, NZ), BF16), pltpu.SMEM((OA,), jnp.int32), vm((OA, NZ), F32), vm((OA, NZ), jnp.int32), vm((2, H, H), BF16),
        vm((32, H), BF16), vm((128, H), BF16), vm((2, H, H), BF16), vm((64, PAIRS), BF16),
        vm((OA, NZ, H), F32), vm((OA, NZ, H), BF16), vm((OA, NZ, H), BF16), vm((OA, NZ, H), BF16),
        vm((H + 16, PAIRS), BF16), vm((H + 16, PAIRS), BF16),
        vm((OA, NZ, H), F32), vm((OA, NZ, H), F32), vm((OA, NZ, H), F32),
        vm((PAIRS, H), BF16), vm((PAIRS, H), BF16), vm((PAIRS, H), BF16), vm((OA, 16, NZ), F32),
        vm((1, 128), F32), vm((ZN, 1, 128), F32), vm((2, 1, 128), F32), vm((XN, 1, 128), F32), vm((2, 8, 128), F32),
        vm((1, 128), F32), vm((ZN, 1, 128), F32), vm((XN, 1, 128), F32), vm((2, 8, 128), F32),
        vm((2, H, 128), F32), vm((2, H + 64, 128), F32), vm((H, 128), F32), vm((H + 64, 128), F32),
        vm((16, 16, 128), F32), vm((16, 20, 128), F32), vm((16, 16, 128), F32), vm((16, 20, 128), F32),
        vm((4, 9, 128), F32), vm((ZN, 9, 128), F32), vm((9, 128), F32), vm((2, YN, XN, 4, 9, 128), F32),
        vm((YN, 24, 128), F32), vm((YN, 24, 128), F32), vm((24, 128), F32), vm((YN, 24, 128), F32),
        dma((5,)), dma((17,)), dma((17,)), dma((4,)), dma((4,)), dma((2 * YN + 1,)),
    ]
    vspec = pl.BlockSpec(memory_space=pltpu.VMEM)
    anyspec = pl.BlockSpec(memory_space=pl.ANY)
    zone, parts = pl.pallas_call(
        kernel,
        out_shape=(
            jax.ShapeDtypeStruct((YN, 24, 128), F32),
            jax.ShapeDtypeStruct((2, YN, XN, 4, 9, 128), F32),
        ),
        in_specs=[anyspec] * 5,
        out_specs=[anyspec] * 2,
        scratch_shapes=shapes,
        compiler_params=pltpu.CompilerParams(
            collective_id=0, has_side_effects=True, vmem_limit_bytes=60 * 2**20
        ),
        name="gravity_backward",
    )(packed, anchor_zone, prior, flows, w_mid)
    out = pl.pallas_call(
        finish,
        out_shape=(
            jax.ShapeDtypeStruct((FZ, NZ), F32),
            jax.ShapeDtypeStruct((2 * FZ + 1, H), F32),
            jax.ShapeDtypeStruct((2, H, H), F32),
            jax.ShapeDtypeStruct((1, H), F32),
            jax.ShapeDtypeStruct((3, H), F32),
        ),
        in_specs=[anyspec] * 2,
        out_specs=[vspec] * 5,
        scratch_shapes=[vm((2, YN, XN, 4, 9, 128), F32), vm((YN, 24, 128), F32), dma((2,))],
        name="results",
    )(parts, zone)
    return out[0], out[1], out[2], out[3].reshape(H), out[4]


def solution(mesh):
    in_specs = (
        P(None, "dest"), P("orig"), P("orig", "dest"), P("orig", "dest"), P("orig", "dest"), P(), P(), P(), P(),
    )
    out_specs = (P(None, "dest"), P(), P(), P(), P())
    return jax.shard_map(
        per_device, mesh=mesh, in_specs=in_specs, out_specs=out_specs, check_vma=False
    )
```

```python
import jax
import jax.numpy as jnp
from jax import lax
from jax.experimental import pallas as pl
from jax.experimental.pallas import tpu as pltpu
from jax.sharding import PartitionSpec as P

MESH = pl.DeviceIdType.MESH
F32 = jnp.float32
BF16 = jnp.bfloat16
XN, ZN, CN, YN = 4, 16, 2, 4
OA, NZ, H, FZ = 4, 512, 256, 19
PAIRS = OA * NZ
FAR = (8, 7, 9, 6, 10, 5, 11, 4, 12, 3, 13, 2, 14, 1, 15)


def nn(a, b):
    return lax.dot_general(a, b, (((1,), (0,)), ((), ())), preferred_element_type=F32)


def nt(a, b):
    return lax.dot_general(a, b, (((1,), (1,)), ((), ())), preferred_element_type=F32)


def tn(a, b):
    return lax.dot_general(a, b, (((0,), (0,)), ((), ())), preferred_element_type=F32)


def iota(shape, dim):
    return lax.broadcasted_iota(jnp.int32, shape, dim)


def total_wait(ref, sem):
    pltpu.make_async_copy(ref, ref, sem).wait()


def send(src, dst, ssem, rsem, device):
    return pltpu.make_async_remote_copy(
        src_ref=src, dst_ref=dst, send_sem=ssem, recv_sem=rsem, device_id=device, device_id_type=MESH
    )


def kernel(
    a_hbm, az_hbm, prior_hbm, flows_hbm, wmid_hbm,
    zout_ref, fout_ref,
    ab, az, prior_v, flows_v, wm,
    wz, w4, wmt, xt, p0, l1, l2, l3, l1t, l2t, g1, g2, g3, d1, d2, d3, scb,
    row1, rows1, rowc1, row2, rows2, rowc2,
    ga, gb, cra, crb, sa, sb, yra, yrb, zs, zr, fp, full, zpart, zpr, zsum, zfull,
    lsem, ssem, rsem, ysem, csem, osem,
):
    dest = lax.axis_index("dest")
    y = lax.axis_index("orig")
    x = dest // (ZN * CN)
    z = (dest // CN) % ZN
    c = dest % CN
    zblk = (z // 4) * 4
    piece = z % 4
    me_q = y * XN + x
    me_p = x * ZN + z

    def dev(x_, z_, c_, y_):
        return ((x_ * ZN + z_) * CN + c_, y_)

    partner = dev(x, z, 1 - c, y)

    barrier = pltpu.get_barrier_semaphore()

    def greet(device):
        pl.semaphore_signal(barrier, inc=1, device_id=device, device_id_type=MESH)

    for t in FAR + (0,):
        for i in (2, 1, 3, 0):
            if t or i:
                greet(dev((x + i) % XN, (z + t) % ZN, c, y))
    for i in range(XN):
        for j in range(1, YN):
            greet(dev((x + i) % XN, z, c, (y + j) % YN))
    greet(partner)

    loads = [
        pltpu.make_async_copy(src, dst, lsem.at[k])
        for k, (src, dst) in enumerate(
            ((a_hbm, ab), (az_hbm, az), (flows_hbm, flows_v), (prior_hbm, prior_v), (wmid_hbm, wm))
        )
    ]
    for cp in loads:
        cp.start()
    for cp in loads:
        cp.wait()

    zfd = ab[0:32].astype(F32)
    dist = zfd[24 : 24 + OA]
    zf32 = jnp.where(iota((32, NZ), 0) < FZ, zfd, 0.0)
    bb = ab[32:80, 0:H].astype(F32)
    worig = jnp.where(iota((32, H), 0) < FZ, bb[0:32], 0.0).astype(BF16)
    wz[...] = jnp.concatenate(
        [bb[FZ : 2 * FZ + 1], bb[40:41], jnp.zeros((32 - FZ - 2, H), F32)], axis=0
    ).astype(BF16)
    w4[...] = jnp.concatenate([worig] * OA, axis=0)
    for k in range(2):
        wmt[k] = wm[k].T
    sub32 = iota((32, NZ), 0)
    for o in range(OA):
        rows = jnp.where(sub32 == FZ, dist[o : o + 1], zf32)
        rows = jnp.where((sub32 == FZ + 1) | (sub32 == 24 + o), 1.0, rows)
        xt[0:32, o * NZ : (o + 1) * NZ] = rows.astype(BF16)
    extra = jnp.where(iota((16, PAIRS), 0) == 0, 1.0, 0.0).astype(BF16)
    l1t[H:, :] = extra
    l2t[H:, :] = extra
    zone_ids = iota((8, NZ), 1) + dest * NZ
    sub8 = iota((8, NZ), 0)
    ids = jnp.full((8, NZ), -1, jnp.int32)
    for o in range(OA):
        ids = jnp.where(sub8 == o, az[o], ids)
    own = (ids == zone_ids).astype(F32).astype(BF16)
    zf4 = jnp.concatenate([zf32.astype(BF16)] * OA, axis=0)
    lane8 = iota((8, 128), 1)
    row8 = iota((8, 128), 0)
    mine = lane8 // 32 == row8
    chosen = nt(own, zf4)
    observed = flows_v[...].astype(F32)
    outflow_here = jnp.sum(observed, axis=1, keepdims=True)
    outflow8 = jnp.concatenate([outflow_here, jnp.zeros((4, 1), F32)], axis=0)
    packed = jnp.where(mine, jnp.where(lane8 % 32 == 31, outflow8, chosen), 0.0)
    row1[...] = jnp.sum(packed, axis=0, keepdims=True)
    for o in range(OA):
        p0[o] = tn(xt[0:32, o * NZ : (o + 1) * NZ], wz[...])

    pl.semaphore_wait(barrier, XN * ZN - 1 + XN * (YN - 1) + 1)

    def plane_start(row, got, s):
        for t in FAR + (0,):
            for i in (2, 1, 3, 0):
                if t or i:
                    device = dev((x + i) % XN, (z + t) % ZN, c, y)
                    send(row, got.at[me_p], ssem.at[s], rsem.at[s], device).start()
        got[me_p] = row[...]

    def core_stage(row, got, s):
        got[0] = jnp.broadcast_to(row, (8, 128))
        send(got.at[0], got.at[1], ssem.at[s], rsem.at[s], partner).start()
        total_wait(got.at[1], rsem.at[s])

    rest = pl.ds(0, XN * ZN - 1)
    plane_start(row1, rows1, 0)
    total_wait(rows1.at[rest], rsem.at[0])
    core_stage(jnp.sum(rows1[...], axis=0), rowc1, 2)
    featrow = rowc1[0] + rowc1[1]
    keep = mine & (lane8 % 32 < FZ)
    cvec = nn(jnp.where(keep, featrow, 0.0).astype(BF16), w4[...])
    outflow = jnp.sum(jnp.where(mine & (lane8 % 32 == 31), featrow, 0.0), axis=1, keepdims=True)

    b1 = bb[41:42]
    b2 = bb[42:43]
    wout = bb[47:48]
    wout16 = jnp.broadcast_to(wout, (16, H)).astype(BF16)

    def act(v):
        s = 0.5 * jnp.tanh(0.5 * v) + 0.5
        l = v * s
        return l.astype(BF16), s + l - l * s

    for o in range(OA):
        a1, k1 = act(p0[o] + cvec[o : o + 1])
        l1[o] = a1
        g1[o] = k1
        a2, k2 = act(nn(a1, wm[0]) + b1)
        l2[o] = a2
        g2[o] = k2
        a3, k3 = act(nn(a2, wm[1]) + b2)
        l3[o] = a3
        g3[o] = k3 * wout
        scb[o] = nt(wout16, a3)

    scores = jnp.zeros((8, NZ), F32)
    for o in range(OA):
        scores = jnp.where(sub8 == o, scb[o, 0:8], scores)
    scores = scores[0:OA] + prior_v[...]
    top = jnp.max(scores, axis=1, keepdims=True)
    part = jnp.sum(jnp.exp(scores - top), axis=1, keepdims=True)
    lane4 = iota((OA, 128), 1)
    row4 = iota((OA, 128), 0)
    row2[...] = jnp.sum(
        jnp.where(lane4 == row4, top, 0.0) + jnp.where(lane4 == row4 + 64, part, 0.0), axis=0, keepdims=True
    )
    plane_start(row2, rows2, 3)

    for o in range(OA):
        l1t[0:H, o * NZ : (o + 1) * NZ] = l1[o].T
        l2t[0:H, o * NZ : (o + 1) * NZ] = l2[o].T
    square = (iota((128, 128), 0) == iota((128, 128), 1)) & (iota((128, 128), 1) % 32 < FZ)
    spread = nn(jnp.where(square, featrow[0:1], 0.0).astype(BF16), jnp.ones((128, NZ), BF16)).astype(BF16)
    for o in range(OA):
        xt[32:64, o * NZ : (o + 1) * NZ] = spread[o * 32 : (o + 1) * 32]

    def merge(stats):
        lane = iota((1, 128), 1)
        moved = pltpu.roll(stats, 64, 1)
        big = jnp.max(stats, axis=0, keepdims=True)
        high = jnp.max(moved, axis=0, keepdims=True)
        factor = jnp.exp(jnp.where(lane >= 64, moved - high, 0.0))
        return jnp.where(lane < 64, big, jnp.sum(stats * factor, axis=0, keepdims=True))

    total_wait(rows2.at[rest], rsem.at[3])
    core_stage(merge(rows2[:, 0, :]), rowc2, 5)
    pair = jnp.where(row8 == 0, rowc2[0], rowc2[1])
    total = jnp.broadcast_to(merge(pair[0:2]), (OA, 128))
    top_all = jnp.sum(jnp.where(lane4 == row4, total, 0.0), axis=1, keepdims=True)
    sum_all = jnp.sum(jnp.where(lane4 == row4 + 64, total, 0.0), axis=1, keepdims=True)
    share = jnp.exp(scores - top_all) / sum_all
    slope = (outflow[0:OA] * share - observed) * (1.0 / 16.0)
    slope16 = jnp.concatenate([slope, jnp.zeros((12, NZ), F32)], axis=0).astype(BF16)

    sub16 = iota((16, H), 0)
    gout = jnp.zeros((8, H), F32)
    for o in range(OA):
        u = tn(slope16, jnp.where(sub16 == o, 1.0, 0.0).astype(BF16))
        d3[o * NZ : (o + 1) * NZ, :] = (u * g3[o]).astype(BF16)
        gout = gout + jnp.sum((u * l3[o].astype(F32)).reshape(NZ // 8, 8, H), axis=0)
    grad_three = nn(l2t[...], d3[...])
    for h in range(2):
        ga[h] = grad_three[0:H, h * 128 : (h + 1) * 128]

    def core_start(src, dst, s):
        n = dst.shape[0] // 4
        for k in range(4):
            span = pl.ds(k * n, n)
            send(src.at[1 - c, span], dst.at[span], ssem.at[s], rsem.at[s], partner).start()

    def y_start(src, dst, s):
        for j in range(1, YN):
            yt_ = (y + j) % YN
            send(src.at[yt_], dst.at[y], ssem.at[s], rsem.at[s], dev(x, z, c, yt_)).start()
        dst[y] = src[y]

    def xy_start(src, dst, s):
        for k in range(1, XN * YN):
            xt_, yt_ = (x + k // YN) % XN, (y + k) % YN
            send(src.at[yt_ * XN + xt_], dst.at[me_q], ssem.at[s], rsem.at[s], dev(xt_, z, c, yt_)).start()
        dst[me_q] = src[me_q]

    three = pl.ds(0, 3)
    fifteen = pl.ds(0, 15)
    core_start(ga, cra, 6)
    for o in range(OA):
        span = slice(o * NZ, (o + 1) * NZ)
        d2[span, :] = (nn(d3[span, :], wmt[1]) * g2[o]).astype(BF16)
    grad_two = nn(l1t[...], d2[...])
    for h in range(2):
        gb[h, 0:H] = grad_two[0:H, h * 128 : (h + 1) * 128]
    total_wait(cra, rsem.at[6])
    sa[...] = (ga[c] + cra[...]).reshape(16, 16, 128)
    xy_start(sa, yra, 7)

    for o in range(OA):
        span = slice(o * NZ, (o + 1) * NZ)
        d1[span, :] = (nn(d2[span, :], wmt[0]) * g1[o]).astype(BF16)
    grad_in = nn(xt[...], d1[...])
    gout = jnp.sum(gout, axis=0, keepdims=True)
    per_anchor = grad_in[24:32]
    high = per_anchor.astype(BF16)
    mid = (per_anchor - high.astype(F32)).astype(BF16)
    term = jnp.where(mine, nt(high, w4[...]) + nt(mid, w4[...]), 0.0)
    tag = jnp.where(mine & (lane8 % 32 == 20) & (dest == 0), ids[:, 0:128].astype(F32), 0.0)
    term = jnp.sum(term + tag, axis=0, keepdims=True)
    row8h = iota((8, H), 0)
    mixed = jnp.where(row8h == 0, grad_two[H : H + 1], 0.0)
    mixed = jnp.where(row8h == 1, grad_three[H : H + 1], mixed)
    mixed = jnp.where(row8h == 2, gout, mixed)
    for h in range(2):
        span = slice(h * 128, (h + 1) * 128)
        gb[h, H : H + 24] = grad_in[0:24, span]
        tile = mixed[:, span]
        if h == 0:
            tile = jnp.where(row8 == 4 + y, term, tile)
        gb[h, H + 24 : H + 32] = tile
        gb[h, H + 32 : H + 64] = grad_in[32:64, span]
    core_start(gb, crb, 8)
    zone = jnp.zeros((32, NZ), F32)
    for o in range(OA):
        zone = zone + nt(wz[...], d1[o * NZ : (o + 1) * NZ, :])
    total_wait(crb, rsem.at[8])
    both = gb[c] + crb[...]
    sb[:, 0:16] = both[0:H].reshape(16, 16, 128)
    sb[:, 16:20] = both[H:].reshape(16, 4, 128)
    xy_start(sb, yrb, 10)
    for j in range(YN):
        zpart[j] = zone[0:24, j * 128 : (j + 1) * 128]
    y_start(zpart, zpr, 9)
    total_wait(zpr.at[three], rsem.at[9])
    zsum[...] = jnp.sum(zpr[...], axis=0)
    for j in range(1, YN):
        send(zsum, zfull.at[y], ssem.at[11], rsem.at[11], dev(x, z, c, (y + j) % YN)).start()
    zfull[y] = zsum[...]
    total_wait(yra.at[fifteen], rsem.at[7])
    sum_a = jnp.sum(yra[...], axis=0)
    total_wait(yrb.at[fifteen], rsem.at[10])
    sum_b = jnp.sum(yrb[...], axis=0)
    zs[0, 0:8] = sum_a[0:8]
    zs[1, 0:8] = sum_a[8:16]
    zs[2, 0:8] = sum_b[0:8]
    zs[3, 0:8] = sum_b[8:16]
    for p in range(4):
        zs[p, 8:9] = sum_b[16 + p : 17 + p]

    for t in FAR:
        zt = (z + t) % ZN
        send(zs.at[zt % 4], zr.at[z], ssem.at[13], rsem.at[13], dev(x, zt, c, y)).start()
    zr[z] = zs[piece]
    total_wait(zr.at[pl.ds(0, ZN - 1)], rsem.at[13])
    fp[...] = jnp.sum(zr[...], axis=0)

    for k in range(1, 4):
        send(fp, full.at[c, y, x, piece], ssem.at[14], rsem.at[14], dev(x, zblk + (z + k) % 4, c, y)).start()
    full[c, y, x, piece] = fp[...]
    total_wait(full.at[c, y, x, three], rsem.at[14])
    block = full.at[c, y, x]
    stores = []
    for i in range(1, XN):
        send(block, block, ssem.at[16], ysem.at[0], dev((x + i) % XN, z, c, y)).start()
    for j in range(1, YN):
        for i in range(XN):
            send(block, block, ssem.at[12], ysem.at[j], dev((x + i) % XN, z, c, (y + j) % YN)).start()
    for j in range(YN):
        yf = (y - j + YN) % YN
        rowset = full.at[c, yf]
        total_wait(rowset if j else full.at[c, yf, three], ysem.at[j])
        send(rowset, rowset, ssem.at[15], csem.at[j], partner).start()
        stores.append(pltpu.make_async_copy(rowset, fout_ref.at[c, yf], osem.at[j]))
        stores[-1].start()
    total_wait(zfull.at[three], rsem.at[11])
    stores.append(pltpu.make_async_copy(zfull, zout_ref, osem.at[2 * YN]))
    stores[-1].start()
    for j in range(YN):
        yf = (y - j + YN) % YN
        total_wait(full.at[1 - c, yf], csem.at[j])
        stores.append(pltpu.make_async_copy(full.at[1 - c, yf], fout_ref.at[1 - c, yf], osem.at[YN + j]))
        stores[-1].start()
    for cp in stores:
        cp.wait()

    for s, ref in (
        (0, rows1.at[rest]), (2, rowc1.at[1]), (3, rows2.at[rest]), (5, rowc2.at[1]),
        (6, cra), (7, yra.at[fifteen]), (8, crb), (9, zpr.at[three]), (10, yrb.at[fifteen]), (11, zfull.at[three]),
        (12, full.at[c, three]), (16, full.at[c, y, three]), (13, zr.at[pl.ds(0, ZN - 1)]), (14, full.at[c, y, x, three]), (15, full.at[c]),
    ):
        total_wait(ref, ssem.at[s])


def finish(f_any, zone_any, zg_ref, gin_ref, gmid_ref, gout_ref, gbias_ref, f_ref, zone_ref, sem):
    dest = lax.axis_index("dest")
    loads = [pltpu.make_async_copy(f_any, f_ref, sem.at[0]), pltpu.make_async_copy(zone_any, zone_ref, sem.at[1])]
    for cp in loads:
        cp.start()
    for cp in loads:
        cp.wait()
    for h in range(2):
        span = slice(h * 128, (h + 1) * 128)
        for q in range(16):
            for p in range(4):
                r = q * 16 + (p % 2) * 8
                gmid_ref[1 - p // 2, r : r + 8, span] = f_ref[h, q // 4, q % 4, p, 0:8]
        small = f_ref[h, :, :, :, 8, :].reshape(64, 128)
        gin_ref[0:FZ, span] = small[32 : 32 + FZ]
        gin_ref[FZ : 2 * FZ + 1, span] = small[0 : FZ + 1]
        gbias_ref[0:1, span] = small[20:21]
        gbias_ref[1:3, span] = small[24:26]
        gout_ref[0:1, span] = small[26:27]
        if h == 0:
            atm = small[28:32]
    table = jnp.concatenate(
        [jnp.concatenate([atm[:, o * 32 : (o + 1) * 32], jnp.zeros((4, 32), F32)], axis=0) for o in range(OA)],
        axis=0,
    )
    hits = (table[:, 20:21] == (iota((32, NZ), 1) + dest * NZ).astype(F32)).astype(F32)
    added = lax.dot_general(
        table, hits, (((0,), (0,)), ((), ())), preferred_element_type=F32, precision=lax.Precision.HIGHEST
    )
    for j in range(YN):
        span = slice(j * 128, (j + 1) * 128)
        zg_ref[:, span] = zone_ref[j, 0:FZ] + added[0:FZ, span]


def per_device(zone_feat, anchor_zone, distance, prior, flows, w_in, w_mid, w_out, biases):
    vm = pltpu.VMEM
    dma = pltpu.SemaphoreType.DMA
    def place(array, row, lane):
        rows, lanes = array.shape
        return lax.pad(array, BF16(0), ((row, 80 - row - rows, 0), (lane, NZ - lane - lanes, 0)))

    packed = place(zone_feat, 0, 0) + place(distance, 24, 0) + place(w_in, 32, 0) + place(biases, 72, 0)
    last = lax.pad(w_out, BF16(0), ((0, NZ - H, 0),))
    packed = packed + jnp.where(iota((80, NZ), 0) == 79, last[None, :], BF16(0))
    shapes = [
        vm((80, NZ), BF16), pltpu.SMEM((OA,), jnp.int32), vm((OA, NZ), F32), vm((OA, NZ), jnp.int32), vm((2, H, H), BF16),
        vm((32, H), BF16), vm((128, H), BF16), vm((2, H, H), BF16), vm((64, PAIRS), BF16),
        vm((OA, NZ, H), F32), vm((OA, NZ, H), BF16), vm((OA, NZ, H), BF16), vm((OA, NZ, H), BF16),
        vm((H + 16, PAIRS), BF16), vm((H + 16, PAIRS), BF16),
        vm((OA, NZ, H), F32), vm((OA, NZ, H), F32), vm((OA, NZ, H), F32),
        vm((PAIRS, H), BF16), vm((PAIRS, H), BF16), vm((PAIRS, H), BF16), vm((OA, 16, NZ), F32),
        vm((1, 128), F32), vm((XN * ZN, 1, 128), F32), vm((2, 8, 128), F32),
        vm((1, 128), F32), vm((XN * ZN, 1, 128), F32), vm((2, 8, 128), F32),
        vm((2, H, 128), F32), vm((2, H + 64, 128), F32), vm((H, 128), F32), vm((H + 64, 128), F32),
        vm((16, 16, 128), F32), vm((16, 20, 128), F32), vm((16, 16, 128), F32), vm((16, 20, 128), F32),
        vm((4, 9, 128), F32), vm((ZN, 9, 128), F32), vm((9, 128), F32), vm((2, YN, XN, 4, 9, 128), F32),
        vm((YN, 24, 128), F32), vm((YN, 24, 128), F32), vm((24, 128), F32), vm((YN, 24, 128), F32),
        dma((5,)), dma((17,)), dma((17,)), dma((4,)), dma((4,)), dma((2 * YN + 1,)),
    ]
    vspec = pl.BlockSpec(memory_space=pltpu.VMEM)
    anyspec = pl.BlockSpec(memory_space=pl.ANY)
    zone, parts = pl.pallas_call(
        kernel,
        out_shape=(
            jax.ShapeDtypeStruct((YN, 24, 128), F32),
            jax.ShapeDtypeStruct((2, YN, XN, 4, 9, 128), F32),
        ),
        in_specs=[anyspec] * 5,
        out_specs=[anyspec] * 2,
        scratch_shapes=shapes,
        compiler_params=pltpu.CompilerParams(
            collective_id=0, has_side_effects=True, vmem_limit_bytes=60 * 2**20
        ),
        name="gravity_backward",
    )(packed, anchor_zone, prior, flows, w_mid)
    out = pl.pallas_call(
        finish,
        out_shape=(
            jax.ShapeDtypeStruct((FZ, NZ), F32),
            jax.ShapeDtypeStruct((2 * FZ + 1, H), F32),
            jax.ShapeDtypeStruct((2, H, H), F32),
            jax.ShapeDtypeStruct((1, H), F32),
            jax.ShapeDtypeStruct((3, H), F32),
        ),
        in_specs=[anyspec] * 2,
        out_specs=[vspec] * 5,
        scratch_shapes=[vm((2, YN, XN, 4, 9, 128), F32), vm((YN, 24, 128), F32), dma((2,))],
        name="results",
    )(parts, zone)
    return out[0], out[1], out[2], out[3].reshape(H), out[4]


def solution(mesh):
    in_specs = (
        P(None, "dest"), P("orig"), P("orig", "dest"), P("orig", "dest"), P("orig", "dest"), P(), P(), P(), P(),
    )
    out_specs = (P(None, "dest"), P(), P(), P(), P())
    return jax.shard_map(
        per_device, mesh=mesh, in_specs=in_specs, out_specs=out_specs, check_vma=False
    )
```

```python
import jax
import jax.numpy as jnp
from jax import lax
from jax.experimental import pallas as pl
from jax.experimental.pallas import tpu as pltpu
from jax.sharding import PartitionSpec as P

MESH = pl.DeviceIdType.MESH
F32 = jnp.float32
BF16 = jnp.bfloat16
XN, ZN, CN, YN = 4, 16, 2, 4
OA, NZ, H, FZ = 4, 512, 256, 19
PAIRS = OA * NZ
FAR = (8, 7, 9, 6, 10, 5, 11, 4, 12, 3, 13, 2, 14, 1, 15)


def nn(a, b):
    return lax.dot_general(a, b, (((1,), (0,)), ((), ())), preferred_element_type=F32)


def nt(a, b):
    return lax.dot_general(a, b, (((1,), (1,)), ((), ())), preferred_element_type=F32)


def tn(a, b):
    return lax.dot_general(a, b, (((0,), (0,)), ((), ())), preferred_element_type=F32)


def iota(shape, dim):
    return lax.broadcasted_iota(jnp.int32, shape, dim)


def total_wait(ref, sem):
    pltpu.make_async_copy(ref, ref, sem).wait()


def send(src, dst, ssem, rsem, device):
    return pltpu.make_async_remote_copy(
        src_ref=src, dst_ref=dst, send_sem=ssem, recv_sem=rsem, device_id=device, device_id_type=MESH
    )


def kernel(
    a_hbm, az_hbm, prior_hbm, flows_hbm, wmid_hbm,
    zout_ref, fout_ref,
    ab, az, prior_v, flows_v, wm,
    wz, w4, wmt, xt, p0, l1, l2, l3, l1t, l2t, g1, g2, g3, d1, d2, d3, scb,
    row1, rows1, rowc1, row2, rows2, rowc2,
    ga, gb, cra, crb, sa, sb, yra, yrb, zs, zr, fp, full, zpart, zpr, zsum, zfull,
    lsem, ssem, rsem, ysem, csem, osem, zsem,
):
    dest = lax.axis_index("dest")
    y = lax.axis_index("orig")
    x = dest // (ZN * CN)
    z = (dest // CN) % ZN
    c = dest % CN
    zblk = (z // 4) * 4
    piece = z % 4
    me_q = y * XN + x
    me_p = x * ZN + z

    def dev(x_, z_, c_, y_):
        return ((x_ * ZN + z_) * CN + c_, y_)

    partner = dev(x, z, 1 - c, y)

    barrier = pltpu.get_barrier_semaphore()

    def greet(device):
        pl.semaphore_signal(barrier, inc=1, device_id=device, device_id_type=MESH)

    for t in FAR + (0,):
        for i in (2, 1, 3, 0):
            if t or i:
                greet(dev((x + i) % XN, (z + t) % ZN, c, y))
    for i in range(XN):
        for j in range(1, YN):
            greet(dev((x + i) % XN, z, c, (y + j) % YN))
    greet(partner)

    loads = [
        pltpu.make_async_copy(src, dst, lsem.at[k])
        for k, (src, dst) in enumerate(
            ((a_hbm, ab), (az_hbm, az), (flows_hbm, flows_v), (prior_hbm, prior_v), (wmid_hbm, wm))
        )
    ]
    for cp in loads:
        cp.start()
    for cp in loads:
        cp.wait()

    zfd = ab[0:32].astype(F32)
    dist = zfd[24 : 24 + OA]
    zf32 = jnp.where(iota((32, NZ), 0) < FZ, zfd, 0.0)
    bb = ab[32:80, 0:H].astype(F32)
    worig = jnp.where(iota((32, H), 0) < FZ, bb[0:32], 0.0).astype(BF16)
    wz[...] = jnp.concatenate(
        [bb[FZ : 2 * FZ + 1], bb[40:41], jnp.zeros((32 - FZ - 2, H), F32)], axis=0
    ).astype(BF16)
    w4[...] = jnp.concatenate([worig] * OA, axis=0)
    for k in range(2):
        wmt[k] = wm[k].T
    sub32 = iota((32, NZ), 0)
    for o in range(OA):
        rows = jnp.where(sub32 == FZ, dist[o : o + 1], zf32)
        rows = jnp.where((sub32 == FZ + 1) | (sub32 == 24 + o), 1.0, rows)
        xt[0:32, o * NZ : (o + 1) * NZ] = rows.astype(BF16)
    extra = jnp.where(iota((16, PAIRS), 0) == 0, 1.0, 0.0).astype(BF16)
    l1t[H:, :] = extra
    l2t[H:, :] = extra
    zone_ids = iota((8, NZ), 1) + dest * NZ
    sub8 = iota((8, NZ), 0)
    ids = jnp.full((8, NZ), -1, jnp.int32)
    for o in range(OA):
        ids = jnp.where(sub8 == o, az[o], ids)
    own = (ids == zone_ids).astype(F32).astype(BF16)
    zf4 = jnp.concatenate([zf32.astype(BF16)] * OA, axis=0)
    lane8 = iota((8, 128), 1)
    row8 = iota((8, 128), 0)
    mine = lane8 // 32 == row8
    chosen = nt(own, zf4)
    observed = flows_v[...].astype(F32)
    outflow_here = jnp.sum(observed, axis=1, keepdims=True)
    outflow8 = jnp.concatenate([outflow_here, jnp.zeros((4, 1), F32)], axis=0)
    packed = jnp.where(mine, jnp.where(lane8 % 32 == 31, outflow8, chosen), 0.0)
    row1[...] = jnp.sum(packed, axis=0, keepdims=True)
    for o in range(OA):
        p0[o] = tn(xt[0:32, o * NZ : (o + 1) * NZ], wz[...])

    pl.semaphore_wait(barrier, XN * ZN - 1 + XN * (YN - 1) + 1)

    def plane_start(row, got, s):
        for t in FAR + (0,):
            for i in (2, 1, 3, 0):
                if t or i:
                    device = dev((x + i) % XN, (z + t) % ZN, c, y)
                    send(row, got.at[me_p], ssem.at[s], rsem.at[s], device).start()
        got[me_p] = row[...]

    def core_stage(row, got, s):
        got[0] = jnp.broadcast_to(row, (8, 128))
        send(got.at[0], got.at[1], ssem.at[s], rsem.at[s], partner).start()
        total_wait(got.at[1], rsem.at[s])

    rest = pl.ds(0, XN * ZN - 1)
    plane_start(row1, rows1, 0)
    total_wait(rows1.at[rest], rsem.at[0])
    core_stage(jnp.sum(rows1[...], axis=0), rowc1, 2)
    featrow = rowc1[0] + rowc1[1]
    keep = mine & (lane8 % 32 < FZ)
    cvec = nn(jnp.where(keep, featrow, 0.0).astype(BF16), w4[...])
    outflow = jnp.sum(jnp.where(mine & (lane8 % 32 == 31), featrow, 0.0), axis=1, keepdims=True)

    b1 = bb[41:42]
    b2 = bb[42:43]
    wout = bb[47:48]
    wout16 = jnp.broadcast_to(wout, (16, H)).astype(BF16)

    def act(v):
        s = 0.5 * jnp.tanh(0.5 * v) + 0.5
        l = v * s
        return l.astype(BF16), s + l - l * s

    for o in range(OA):
        a1, k1 = act(p0[o] + cvec[o : o + 1])
        l1[o] = a1
        g1[o] = k1
        a2, k2 = act(nn(a1, wm[0]) + b1)
        l2[o] = a2
        g2[o] = k2
        a3, k3 = act(nn(a2, wm[1]) + b2)
        l3[o] = a3
        g3[o] = k3 * wout
        scb[o] = nt(wout16, a3)

    scores = jnp.zeros((8, NZ), F32)
    for o in range(OA):
        scores = jnp.where(sub8 == o, scb[o, 0:8], scores)
    scores = scores[0:OA] + prior_v[...]
    top = jnp.max(scores, axis=1, keepdims=True)
    part = jnp.sum(jnp.exp(scores - top), axis=1, keepdims=True)
    lane4 = iota((OA, 128), 1)
    row4 = iota((OA, 128), 0)
    row2[...] = jnp.sum(
        jnp.where(lane4 == row4, top, 0.0) + jnp.where(lane4 == row4 + 64, part, 0.0), axis=0, keepdims=True
    )
    plane_start(row2, rows2, 3)

    for o in range(OA):
        l1t[0:H, o * NZ : (o + 1) * NZ] = l1[o].T
        l2t[0:H, o * NZ : (o + 1) * NZ] = l2[o].T
    square = (iota((128, 128), 0) == iota((128, 128), 1)) & (iota((128, 128), 1) % 32 < FZ)
    spread = nn(jnp.where(square, featrow[0:1], 0.0).astype(BF16), jnp.ones((128, NZ), BF16)).astype(BF16)
    for o in range(OA):
        xt[32:64, o * NZ : (o + 1) * NZ] = spread[o * 32 : (o + 1) * 32]

    def merge(stats):
        lane = iota((1, 128), 1)
        moved = pltpu.roll(stats, 64, 1)
        big = jnp.max(stats, axis=0, keepdims=True)
        high = jnp.max(moved, axis=0, keepdims=True)
        factor = jnp.exp(jnp.where(lane >= 64, moved - high, 0.0))
        return jnp.where(lane < 64, big, jnp.sum(stats * factor, axis=0, keepdims=True))

    total_wait(rows2.at[rest], rsem.at[3])
    core_stage(merge(rows2[:, 0, :]), rowc2, 5)
    pair = jnp.where(row8 == 0, rowc2[0], rowc2[1])
    total = jnp.broadcast_to(merge(pair[0:2]), (OA, 128))
    top_all = jnp.sum(jnp.where(lane4 == row4, total, 0.0), axis=1, keepdims=True)
    sum_all = jnp.sum(jnp.where(lane4 == row4 + 64, total, 0.0), axis=1, keepdims=True)
    share = jnp.exp(scores - top_all) / sum_all
    slope = (outflow[0:OA] * share - observed) * (1.0 / 16.0)
    slope16 = jnp.concatenate([slope, jnp.zeros((12, NZ), F32)], axis=0).astype(BF16)

    sub16 = iota((16, H), 0)
    gout = jnp.zeros((8, H), F32)
    for o in range(OA):
        u = tn(slope16, jnp.where(sub16 == o, 1.0, 0.0).astype(BF16))
        d3[o * NZ : (o + 1) * NZ, :] = (u * g3[o]).astype(BF16)
        gout = gout + jnp.sum((u * l3[o].astype(F32)).reshape(NZ // 8, 8, H), axis=0)
    grad_three = nn(l2t[...], d3[...])
    for h in range(2):
        ga[h] = grad_three[0:H, h * 128 : (h + 1) * 128]

    def core_start(src, dst, s):
        n = dst.shape[0] // 4
        for k in range(4):
            span = pl.ds(k * n, n)
            send(src.at[1 - c, span], dst.at[span], ssem.at[s], rsem.at[s], partner).start()

    def y_start(src, dst, s):
        for j in range(1, YN):
            yt_ = (y + j) % YN
            send(src.at[yt_], dst.at[y], ssem.at[s], rsem.at[s], dev(x, z, c, yt_)).start()
        dst[y] = src[y]

    def xy_start(src, dst, s):
        for k in range(1, XN * YN):
            xt_, yt_ = (x + k // YN) % XN, (y + k) % YN
            send(src.at[yt_ * XN + xt_], dst.at[me_q], ssem.at[s], rsem.at[s], dev(xt_, z, c, yt_)).start()
        dst[me_q] = src[me_q]

    three = pl.ds(0, 3)
    fifteen = pl.ds(0, 15)
    core_start(ga, cra, 6)
    for o in range(OA):
        span = slice(o * NZ, (o + 1) * NZ)
        d2[span, :] = (nn(d3[span, :], wmt[1]) * g2[o]).astype(BF16)
    grad_two = nn(l1t[...], d2[...])
    for h in range(2):
        gb[h, 0:H] = grad_two[0:H, h * 128 : (h + 1) * 128]
    total_wait(cra, rsem.at[6])
    sa[...] = (ga[c] + cra[...]).reshape(16, 16, 128)
    xy_start(sa, yra, 7)

    for o in range(OA):
        span = slice(o * NZ, (o + 1) * NZ)
        d1[span, :] = (nn(d2[span, :], wmt[0]) * g1[o]).astype(BF16)
    grad_in = nn(xt[...], d1[...])
    gout = jnp.sum(gout, axis=0, keepdims=True)
    per_anchor = grad_in[24:32]
    high = per_anchor.astype(BF16)
    mid = (per_anchor - high.astype(F32)).astype(BF16)
    term = jnp.where(mine, nt(high, w4[...]) + nt(mid, w4[...]), 0.0)
    tag = jnp.where(mine & (lane8 % 32 == 20) & (dest == 0), ids[:, 0:128].astype(F32), 0.0)
    term = jnp.sum(term + tag, axis=0, keepdims=True)
    row8h = iota((8, H), 0)
    mixed = jnp.where(row8h == 0, grad_two[H : H + 1], 0.0)
    mixed = jnp.where(row8h == 1, grad_three[H : H + 1], mixed)
    mixed = jnp.where(row8h == 2, gout, mixed)
    for h in range(2):
        span = slice(h * 128, (h + 1) * 128)
        gb[h, H : H + 24] = grad_in[0:24, span]
        tile = mixed[:, span]
        if h == 0:
            tile = jnp.where(row8 == 4 + y, term, tile)
        gb[h, H + 24 : H + 32] = tile
        gb[h, H + 32 : H + 64] = grad_in[32:64, span]
    core_start(gb, crb, 8)
    zone = jnp.zeros((32, NZ), F32)
    for o in range(OA):
        zone = zone + nt(wz[...], d1[o * NZ : (o + 1) * NZ, :])
    total_wait(crb, rsem.at[8])
    both = gb[c] + crb[...]
    sb[:, 0:16] = both[0:H].reshape(16, 16, 128)
    sb[:, 16:20] = both[H:].reshape(16, 4, 128)
    xy_start(sb, yrb, 10)
    for j in range(YN):
        zpart[j] = zone[0:24, j * 128 : (j + 1) * 128]
    y_start(zpart, zpr, 9)
    total_wait(zpr.at[three], rsem.at[9])
    zsum[...] = jnp.sum(zpr[...], axis=0)
    for j in range(1, YN):
        send(zsum, zfull.at[y], ssem.at[11], rsem.at[11], dev(x, z, c, (y + j) % YN)).start()
    zfull[y] = zsum[...]
    total_wait(yra.at[fifteen], rsem.at[7])
    sum_a = jnp.sum(yra[...], axis=0)
    total_wait(yrb.at[fifteen], rsem.at[10])
    sum_b = jnp.sum(yrb[...], axis=0)
    zs[0, 0:8] = sum_a[0:8]
    zs[1, 0:8] = sum_a[8:16]
    zs[2, 0:8] = sum_b[0:8]
    zs[3, 0:8] = sum_b[8:16]
    for p in range(4):
        zs[p, 8:9] = sum_b[16 + p : 17 + p]

    for t in FAR:
        zt = (z + t) % ZN
        send(zs.at[zt % 4], zr.at[z], ssem.at[13], rsem.at[13], dev(x, zt, c, y)).start()
    zr[z] = zs[piece]
    total_wait(zr.at[pl.ds(0, ZN - 1)], rsem.at[13])
    fp[...] = jnp.sum(zr[...], axis=0)

    for k in range(1, 4):
        send(fp, full.at[c, y, x, piece], ssem.at[14], zsem.at[k], dev(x, zblk + (z + k) % 4, c, y)).start()
    full[c, y, x, piece] = fp[...]
    stores = []
    upper = piece // 2
    for n, pk in enumerate((piece, piece + 1 - 2 * (piece % 2), 2 - upper, 3 - 3 * upper)):
        block = full.at[c, y, x, pk]
        if n:
            total_wait(block, zsem.at[(piece - pk + 4) % 4])
        for j in range(1, YN):
            for i in range(XN):
                send(block, block, ssem.at[12], ysem.at[j], dev((x + i) % XN, z, c, (y + j) % YN)).start()
        for i in range(1, XN):
            send(block, block, ssem.at[16], ysem.at[0], dev((x + i) % XN, z, c, y)).start()
    for j in range(YN):
        yf = (y - j + YN) % YN
        rowset = full.at[c, yf]
        total_wait(rowset if j else full.at[c, yf, three], ysem.at[j])
        send(rowset, rowset, ssem.at[15], csem.at[j], partner).start()
        stores.append(pltpu.make_async_copy(rowset, fout_ref.at[c, yf], osem.at[j]))
        stores[-1].start()
    total_wait(zfull.at[three], rsem.at[11])
    stores.append(pltpu.make_async_copy(zfull, zout_ref, osem.at[2 * YN]))
    stores[-1].start()
    for j in range(YN):
        yf = (y - j + YN) % YN
        total_wait(full.at[1 - c, yf], csem.at[j])
        stores.append(pltpu.make_async_copy(full.at[1 - c, yf], fout_ref.at[1 - c, yf], osem.at[YN + j]))
        stores[-1].start()
    for cp in stores:
        cp.wait()

    for s, ref in (
        (0, rows1.at[rest]), (2, rowc1.at[1]), (3, rows2.at[rest]), (5, rowc2.at[1]),
        (6, cra), (7, yra.at[fifteen]), (8, crb), (9, zpr.at[three]), (10, yrb.at[fifteen]), (11, zfull.at[three]),
        (12, full.at[c, three]), (16, full.at[c, y, three]), (13, zr.at[pl.ds(0, ZN - 1)]), (14, full.at[c, y, x, three]), (15, full.at[c]),
    ):
        total_wait(ref, ssem.at[s])


def finish(f_any, zone_any, zg_ref, gin_ref, gmid_ref, gout_ref, gbias_ref, f_ref, zone_ref, sem):
    dest = lax.axis_index("dest")
    loads = [pltpu.make_async_copy(f_any, f_ref, sem.at[0]), pltpu.make_async_copy(zone_any, zone_ref, sem.at[1])]
    for cp in loads:
        cp.start()
    for cp in loads:
        cp.wait()
    for h in range(2):
        span = slice(h * 128, (h + 1) * 128)
        for q in range(16):
            for p in range(4):
                r = q * 16 + (p % 2) * 8
                gmid_ref[1 - p // 2, r : r + 8, span] = f_ref[h, q // 4, q % 4, p, 0:8]
        small = f_ref[h, :, :, :, 8, :].reshape(64, 128)
        gin_ref[0:FZ, span] = small[32 : 32 + FZ]
        gin_ref[FZ : 2 * FZ + 1, span] = small[0 : FZ + 1]
        gbias_ref[0:1, span] = small[20:21]
        gbias_ref[1:3, span] = small[24:26]
        gout_ref[0:1, span] = small[26:27]
        if h == 0:
            atm = small[28:32]
    table = jnp.concatenate(
        [jnp.concatenate([atm[:, o * 32 : (o + 1) * 32], jnp.zeros((4, 32), F32)], axis=0) for o in range(OA)],
        axis=0,
    )
    hits = (table[:, 20:21] == (iota((32, NZ), 1) + dest * NZ).astype(F32)).astype(F32)
    added = lax.dot_general(
        table, hits, (((0,), (0,)), ((), ())), preferred_element_type=F32, precision=lax.Precision.HIGHEST
    )
    for j in range(YN):
        span = slice(j * 128, (j + 1) * 128)
        zg_ref[:, span] = zone_ref[j, 0:FZ] + added[0:FZ, span]


def per_device(zone_feat, anchor_zone, distance, prior, flows, w_in, w_mid, w_out, biases):
    vm = pltpu.VMEM
    dma = pltpu.SemaphoreType.DMA
    def place(array, row, lane):
        rows, lanes = array.shape
        return lax.pad(array, BF16(0), ((row, 80 - row - rows, 0), (lane, NZ - lane - lanes, 0)))

    packed = place(zone_feat, 0, 0) + place(distance, 24, 0) + place(w_in, 32, 0) + place(biases, 72, 0)
    last = lax.pad(w_out, BF16(0), ((0, NZ - H, 0),))
    packed = packed + jnp.where(iota((80, NZ), 0) == 79, last[None, :], BF16(0))
    shapes = [
        vm((80, NZ), BF16), pltpu.SMEM((OA,), jnp.int32), vm((OA, NZ), F32), vm((OA, NZ), jnp.int32), vm((2, H, H), BF16),
        vm((32, H), BF16), vm((128, H), BF16), vm((2, H, H), BF16), vm((64, PAIRS), BF16),
        vm((OA, NZ, H), F32), vm((OA, NZ, H), BF16), vm((OA, NZ, H), BF16), vm((OA, NZ, H), BF16),
        vm((H + 16, PAIRS), BF16), vm((H + 16, PAIRS), BF16),
        vm((OA, NZ, H), F32), vm((OA, NZ, H), F32), vm((OA, NZ, H), F32),
        vm((PAIRS, H), BF16), vm((PAIRS, H), BF16), vm((PAIRS, H), BF16), vm((OA, 16, NZ), F32),
        vm((1, 128), F32), vm((XN * ZN, 1, 128), F32), vm((2, 8, 128), F32),
        vm((1, 128), F32), vm((XN * ZN, 1, 128), F32), vm((2, 8, 128), F32),
        vm((2, H, 128), F32), vm((2, H + 64, 128), F32), vm((H, 128), F32), vm((H + 64, 128), F32),
        vm((16, 16, 128), F32), vm((16, 20, 128), F32), vm((16, 16, 128), F32), vm((16, 20, 128), F32),
        vm((4, 9, 128), F32), vm((ZN, 9, 128), F32), vm((9, 128), F32), vm((2, YN, XN, 4, 9, 128), F32),
        vm((YN, 24, 128), F32), vm((YN, 24, 128), F32), vm((24, 128), F32), vm((YN, 24, 128), F32),
        dma((5,)), dma((17,)), dma((17,)), dma((4,)), dma((4,)), dma((2 * YN + 1,)), dma((4,)),
    ]
    vspec = pl.BlockSpec(memory_space=pltpu.VMEM)
    anyspec = pl.BlockSpec(memory_space=pl.ANY)
    zone, parts = pl.pallas_call(
        kernel,
        out_shape=(
            jax.ShapeDtypeStruct((YN, 24, 128), F32),
            jax.ShapeDtypeStruct((2, YN, XN, 4, 9, 128), F32),
        ),
        in_specs=[anyspec] * 5,
        out_specs=[anyspec] * 2,
        scratch_shapes=shapes,
        compiler_params=pltpu.CompilerParams(
            collective_id=0, has_side_effects=True, vmem_limit_bytes=60 * 2**20
        ),
        name="gravity_backward",
    )(packed, anchor_zone, prior, flows, w_mid)
    out = pl.pallas_call(
        finish,
        out_shape=(
            jax.ShapeDtypeStruct((FZ, NZ), F32),
            jax.ShapeDtypeStruct((2 * FZ + 1, H), F32),
            jax.ShapeDtypeStruct((2, H, H), F32),
            jax.ShapeDtypeStruct((1, H), F32),
            jax.ShapeDtypeStruct((3, H), F32),
        ),
        in_specs=[anyspec] * 2,
        out_specs=[vspec] * 5,
        scratch_shapes=[vm((2, YN, XN, 4, 9, 128), F32), vm((YN, 24, 128), F32), dma((2,))],
        name="results",
    )(parts, zone)
    return out[0], out[1], out[2], out[3].reshape(H), out[4]


def solution(mesh):
    in_specs = (
        P(None, "dest"), P("orig"), P("orig", "dest"), P("orig", "dest"), P("orig", "dest"), P(), P(), P(), P(),
    )
    out_specs = (P(None, "dest"), P(), P(), P(), P())
    return jax.shard_map(
        per_device, mesh=mesh, in_specs=in_specs, out_specs=out_specs, check_vma=False
    )
```

```python
import jax
import jax.numpy as jnp
from jax import lax
from jax.experimental import pallas as pl
from jax.experimental.pallas import tpu as pltpu
from jax.sharding import PartitionSpec as P

MESH = pl.DeviceIdType.MESH
F32 = jnp.float32
BF16 = jnp.bfloat16
XN, ZN, CN, YN = 4, 16, 2, 4
OA, NZ, H, FZ = 4, 512, 256, 19
PAIRS = OA * NZ
FAR = (8, 7, 9, 6, 10, 5, 11, 4, 12, 3, 13, 2, 14, 1, 15)


def nn(a, b):
    return lax.dot_general(a, b, (((1,), (0,)), ((), ())), preferred_element_type=F32)


def nt(a, b):
    return lax.dot_general(a, b, (((1,), (1,)), ((), ())), preferred_element_type=F32)


def tn(a, b):
    return lax.dot_general(a, b, (((0,), (0,)), ((), ())), preferred_element_type=F32)


def iota(shape, dim):
    return lax.broadcasted_iota(jnp.int32, shape, dim)


def total_wait(ref, sem):
    pltpu.make_async_copy(ref, ref, sem).wait()


def send(src, dst, ssem, rsem, device):
    return pltpu.make_async_remote_copy(
        src_ref=src, dst_ref=dst, send_sem=ssem, recv_sem=rsem, device_id=device, device_id_type=MESH
    )


def kernel(
    a_hbm, az_hbm, prior_hbm, flows_hbm, wmid_hbm,
    zout_ref, fout_ref,
    ab, az, prior_v, flows_v, wm,
    wz, w4, wmt, xt, p0, l1, l2, l3, l1t, l2t, g1, g2, g3, d1, d2, d3, scb,
    row1, rows1, rowc1, row2, rows2, rowc2,
    ga, gb, cra, crb, sa, sb, yra, yrb, zs, zr, fp, full, zpart, zpr, zsum, zfull,
    lsem, ssem, rsem, ysem, csem, osem, zsem,
):
    dest = lax.axis_index("dest")
    y = lax.axis_index("orig")
    x = dest // (ZN * CN)
    z = (dest // CN) % ZN
    c = dest % CN
    zblk = (z // 4) * 4
    piece = z % 4
    me_q = y * XN + x
    me_p = x * ZN + z

    def dev(x_, z_, c_, y_):
        return ((x_ * ZN + z_) * CN + c_, y_)

    partner = dev(x, z, 1 - c, y)

    barrier = pltpu.get_barrier_semaphore()

    def greet(device):
        pl.semaphore_signal(barrier, inc=1, device_id=device, device_id_type=MESH)

    for t in FAR + (0,):
        for i in (2, 1, 3, 0):
            if t or i:
                greet(dev((x + i) % XN, (z + t) % ZN, c, y))
    for i in range(XN):
        for j in range(1, YN):
            greet(dev((x + i) % XN, z, c, (y + j) % YN))
    greet(partner)

    loads = [
        pltpu.make_async_copy(src, dst, lsem.at[k])
        for k, (src, dst) in enumerate(
            ((a_hbm, ab), (az_hbm, az), (flows_hbm, flows_v), (prior_hbm, prior_v), (wmid_hbm, wm))
        )
    ]
    for cp in loads:
        cp.start()
    for cp in loads:
        cp.wait()

    zfd = ab[0:32].astype(F32)
    dist = zfd[24 : 24 + OA]
    zf32 = jnp.where(iota((32, NZ), 0) < FZ, zfd, 0.0)
    bb = ab[32:80, 0:H].astype(F32)
    worig = jnp.where(iota((32, H), 0) < FZ, bb[0:32], 0.0).astype(BF16)
    wz[...] = jnp.concatenate(
        [bb[FZ : 2 * FZ + 1], bb[40:41], jnp.zeros((32 - FZ - 2, H), F32)], axis=0
    ).astype(BF16)
    w4[...] = jnp.concatenate([worig] * OA, axis=0)
    for k in range(2):
        wmt[k] = wm[k].T
    sub32 = iota((32, NZ), 0)
    for o in range(OA):
        rows = jnp.where(sub32 == FZ, dist[o : o + 1], zf32)
        rows = jnp.where((sub32 == FZ + 1) | (sub32 == 24 + o), 1.0, rows)
        xt[0:32, o * NZ : (o + 1) * NZ] = rows.astype(BF16)
    extra = jnp.where(iota((16, PAIRS), 0) == 0, 1.0, 0.0).astype(BF16)
    l1t[H:, :] = extra
    l2t[H:, :] = extra
    zone_ids = iota((8, NZ), 1) + dest * NZ
    sub8 = iota((8, NZ), 0)
    ids = jnp.full((8, NZ), -1, jnp.int32)
    for o in range(OA):
        ids = jnp.where(sub8 == o, az[o], ids)
    own = (ids == zone_ids).astype(F32).astype(BF16)
    zf4 = jnp.concatenate([zf32.astype(BF16)] * OA, axis=0)
    lane8 = iota((8, 128), 1)
    row8 = iota((8, 128), 0)
    mine = lane8 // 32 == row8
    chosen = nt(own, zf4)
    observed = flows_v[...].astype(F32)
    outflow_here = jnp.sum(observed, axis=1, keepdims=True)
    outflow8 = jnp.concatenate([outflow_here, jnp.zeros((4, 1), F32)], axis=0)
    packed = jnp.where(mine, jnp.where(lane8 % 32 == 31, outflow8, chosen), 0.0)
    row1[...] = jnp.sum(packed, axis=0, keepdims=True)
    for o in range(OA):
        p0[o] = tn(xt[0:32, o * NZ : (o + 1) * NZ], wz[...])

    pl.semaphore_wait(barrier, XN * ZN - 1 + XN * (YN - 1) + 1)

    def plane_start(row, got, s):
        for t in FAR + (0,):
            for i in (2, 1, 3, 0):
                if t or i:
                    device = dev((x + i) % XN, (z + t) % ZN, c, y)
                    send(row, got.at[me_p], ssem.at[s], rsem.at[s], device).start()
        got[me_p] = row[...]

    def core_stage(row, got, s):
        got[0] = jnp.broadcast_to(row, (8, 128))
        send(got.at[0], got.at[1], ssem.at[s], rsem.at[s], partner).start()
        total_wait(got.at[1], rsem.at[s])

    rest = pl.ds(0, XN * ZN - 1)
    plane_start(row1, rows1, 0)
    total_wait(rows1.at[rest], rsem.at[0])
    core_stage(jnp.sum(rows1[...], axis=0), rowc1, 2)
    featrow = rowc1[0] + rowc1[1]
    keep = mine & (lane8 % 32 < FZ)
    cvec = nn(jnp.where(keep, featrow, 0.0).astype(BF16), w4[...])
    outflow = jnp.sum(jnp.where(mine & (lane8 % 32 == 31), featrow, 0.0), axis=1, keepdims=True)

    b1 = bb[41:42]
    b2 = bb[42:43]
    wout = bb[47:48]
    wout16 = jnp.broadcast_to(wout, (16, H)).astype(BF16)

    def act(v):
        s = 0.5 * jnp.tanh(0.5 * v) + 0.5
        l = v * s
        return l.astype(BF16), s + l - l * s

    for o in range(OA):
        a1, k1 = act(p0[o] + cvec[o : o + 1])
        l1[o] = a1
        g1[o] = k1
        a2, k2 = act(nn(a1, wm[0]) + b1)
        l2[o] = a2
        g2[o] = k2
        a3, k3 = act(nn(a2, wm[1]) + b2)
        l3[o] = a3
        g3[o] = k3 * wout
        scb[o] = nt(wout16, a3)

    scores = jnp.zeros((8, NZ), F32)
    for o in range(OA):
        scores = jnp.where(sub8 == o, scb[o, 0:8], scores)
    scores = scores[0:OA] + prior_v[...]
    top = jnp.max(scores, axis=1, keepdims=True)
    part = jnp.sum(jnp.exp(scores - top), axis=1, keepdims=True)
    lane4 = iota((OA, 128), 1)
    row4 = iota((OA, 128), 0)
    row2[...] = jnp.sum(
        jnp.where(lane4 == row4, top, 0.0) + jnp.where(lane4 == row4 + 64, part, 0.0), axis=0, keepdims=True
    )
    plane_start(row2, rows2, 3)

    for o in range(OA):
        l1t[0:H, o * NZ : (o + 1) * NZ] = l1[o].T
        l2t[0:H, o * NZ : (o + 1) * NZ] = l2[o].T
    square = (iota((128, 128), 0) == iota((128, 128), 1)) & (iota((128, 128), 1) % 32 < FZ)
    spread = nn(jnp.where(square, featrow[0:1], 0.0).astype(BF16), jnp.ones((128, NZ), BF16)).astype(BF16)
    for o in range(OA):
        xt[32:64, o * NZ : (o + 1) * NZ] = spread[o * 32 : (o + 1) * 32]

    def merge(stats):
        lane = iota((1, 128), 1)
        moved = pltpu.roll(stats, 64, 1)
        big = jnp.max(stats, axis=0, keepdims=True)
        high = jnp.max(moved, axis=0, keepdims=True)
        factor = jnp.exp(jnp.where(lane >= 64, moved - high, 0.0))
        return jnp.where(lane < 64, big, jnp.sum(stats * factor, axis=0, keepdims=True))

    total_wait(rows2.at[rest], rsem.at[3])
    core_stage(merge(rows2[:, 0, :]), rowc2, 5)
    pair = jnp.where(row8 == 0, rowc2[0], rowc2[1])
    total = jnp.broadcast_to(merge(pair[0:2]), (OA, 128))
    top_all = jnp.sum(jnp.where(lane4 == row4, total, 0.0), axis=1, keepdims=True)
    sum_all = jnp.sum(jnp.where(lane4 == row4 + 64, total, 0.0), axis=1, keepdims=True)
    share = jnp.exp(scores - top_all) / sum_all
    slope = (outflow[0:OA] * share - observed) * (1.0 / 16.0)
    slope16 = jnp.concatenate([slope, jnp.zeros((12, NZ), F32)], axis=0).astype(BF16)

    sub16 = iota((16, H), 0)
    gout = jnp.zeros((8, H), F32)
    for o in range(OA):
        u = tn(slope16, jnp.where(sub16 == o, 1.0, 0.0).astype(BF16))
        d3[o * NZ : (o + 1) * NZ, :] = (u * g3[o]).astype(BF16)
        gout = gout + jnp.sum((u * l3[o].astype(F32)).reshape(NZ // 8, 8, H), axis=0)
    grad_three = nn(l2t[...], d3[...])
    for h in range(2):
        ga[h] = grad_three[0:H, h * 128 : (h + 1) * 128]

    def core_start(src, dst, s):
        n = dst.shape[0] // 4
        for k in range(4):
            span = pl.ds(k * n, n)
            send(src.at[1 - c, span], dst.at[span], ssem.at[s], rsem.at[s], partner).start()

    def y_start(src, dst, s):
        for j in range(1, YN):
            yt_ = (y + j) % YN
            send(src.at[yt_], dst.at[y], ssem.at[s], rsem.at[s], dev(x, z, c, yt_)).start()
        dst[y] = src[y]

    def xy_start(src, dst, s):
        for k in range(1, XN * YN):
            xt_, yt_ = (x + k // YN) % XN, (y + k) % YN
            send(src.at[yt_ * XN + xt_], dst.at[me_q], ssem.at[s], rsem.at[s], dev(xt_, z, c, yt_)).start()
        dst[me_q] = src[me_q]

    three = pl.ds(0, 3)
    fifteen = pl.ds(0, 15)
    core_start(ga, cra, 6)
    for o in range(OA):
        span = slice(o * NZ, (o + 1) * NZ)
        d2[span, :] = (nn(d3[span, :], wmt[1]) * g2[o]).astype(BF16)
    grad_two = nn(l1t[...], d2[...])
    for h in range(2):
        gb[h, 0:H] = grad_two[0:H, h * 128 : (h + 1) * 128]
    total_wait(cra, rsem.at[6])
    sa[...] = (ga[c] + cra[...]).reshape(16, 16, 128)
    xy_start(sa, yra, 7)

    for o in range(OA):
        span = slice(o * NZ, (o + 1) * NZ)
        d1[span, :] = (nn(d2[span, :], wmt[0]) * g1[o]).astype(BF16)
    grad_in = nn(xt[...], d1[...])
    gout = jnp.sum(gout, axis=0, keepdims=True)
    per_anchor = grad_in[24:32]
    high = per_anchor.astype(BF16)
    mid = (per_anchor - high.astype(F32)).astype(BF16)
    term = jnp.where(mine, nt(high, w4[...]) + nt(mid, w4[...]), 0.0)
    tag = jnp.where(mine & (lane8 % 32 == 20) & (dest == 0), ids[:, 0:128].astype(F32), 0.0)
    term = jnp.sum(term + tag, axis=0, keepdims=True)
    row8h = iota((8, H), 0)
    mixed = jnp.where(row8h == 0, grad_two[H : H + 1], 0.0)
    mixed = jnp.where(row8h == 1, grad_three[H : H + 1], mixed)
    mixed = jnp.where(row8h == 2, gout, mixed)
    for h in range(2):
        span = slice(h * 128, (h + 1) * 128)
        gb[h, H : H + 24] = grad_in[0:24, span]
        tile = mixed[:, span]
        if h == 0:
            tile = jnp.where(row8 == 4 + y, term, tile)
        gb[h, H + 24 : H + 32] = tile
        gb[h, H + 32 : H + 64] = grad_in[32:64, span]
    core_start(gb, crb, 8)
    zone = jnp.zeros((32, NZ), F32)
    for o in range(OA):
        zone = zone + nt(wz[...], d1[o * NZ : (o + 1) * NZ, :])
    total_wait(crb, rsem.at[8])
    both = gb[c] + crb[...]
    sb[:, 0:16] = both[0:H].reshape(16, 16, 128)
    sb[:, 16:20] = both[H:].reshape(16, 4, 128)
    xy_start(sb, yrb, 10)
    for j in range(YN):
        zpart[j] = zone[0:24, j * 128 : (j + 1) * 128]
    y_start(zpart, zpr, 9)
    total_wait(zpr.at[three], rsem.at[9])
    zsum[...] = jnp.sum(zpr[...], axis=0)
    for j in range(1, YN):
        send(zsum, zfull.at[y], ssem.at[11], rsem.at[11], dev(x, z, c, (y + j) % YN)).start()
    zfull[y] = zsum[...]
    total_wait(yra.at[fifteen], rsem.at[7])
    sum_a = jnp.sum(yra[...], axis=0)
    total_wait(yrb.at[fifteen], rsem.at[10])
    sum_b = jnp.sum(yrb[...], axis=0)
    zs[0, 0:8] = sum_a[0:8]
    zs[1, 0:8] = sum_a[8:16]
    zs[2, 0:8] = sum_b[0:8]
    zs[3, 0:8] = sum_b[8:16]
    for p in range(4):
        zs[p, 8:9] = sum_b[16 + p : 17 + p]

    for t in FAR:
        zt = (z + t) % ZN
        send(zs.at[zt % 4], zr.at[z], ssem.at[13], rsem.at[13], dev(x, zt, c, y)).start()
    zr[z] = zs[piece]
    total_wait(zr.at[pl.ds(0, ZN - 1)], rsem.at[13])
    fp[...] = jnp.sum(zr[...], axis=0)

    for k in range(1, 4):
        send(fp, full.at[c, y, x, piece], ssem.at[14], zsem.at[k], dev(x, zblk + (z + k) % 4, c, y)).start()
    full[c, y, x, piece] = fp[...]
    stores = []
    upper = piece // 2
    for n, pk in enumerate((piece, piece + 1 - 2 * (piece % 2), 2 - upper, 3 - 3 * upper)):
        block = full.at[c, y, x, pk]
        if n:
            total_wait(block, zsem.at[(piece - pk + 4) % 4])
        for i in range(1, XN):
            send(block, block, ssem.at[16], ysem.at[0], dev((x + i) % XN, z, c, y)).start()
        for j in range(1, YN):
            for i in range(XN):
                send(block, block, ssem.at[12], ysem.at[j], dev((x + i) % XN, z, c, (y + j) % YN)).start()
    for j in range(YN):
        yf = (y - j + YN) % YN
        rowset = full.at[c, yf]
        total_wait(rowset if j else full.at[c, yf, three], ysem.at[j])
        send(rowset, rowset, ssem.at[15], csem.at[j], partner).start()
        stores.append(pltpu.make_async_copy(rowset, fout_ref.at[c, yf], osem.at[j]))
        stores[-1].start()
    total_wait(zfull.at[three], rsem.at[11])
    stores.append(pltpu.make_async_copy(zfull, zout_ref, osem.at[2 * YN]))
    stores[-1].start()
    for j in range(YN):
        yf = (y - j + YN) % YN
        total_wait(full.at[1 - c, yf], csem.at[j])
        stores.append(pltpu.make_async_copy(full.at[1 - c, yf], fout_ref.at[1 - c, yf], osem.at[YN + j]))
        stores[-1].start()
    for cp in stores:
        cp.wait()

    for s, ref in (
        (0, rows1.at[rest]), (2, rowc1.at[1]), (3, rows2.at[rest]), (5, rowc2.at[1]),
        (6, cra), (7, yra.at[fifteen]), (8, crb), (9, zpr.at[three]), (10, yrb.at[fifteen]), (11, zfull.at[three]),
        (12, full.at[c, three]), (16, full.at[c, y, three]), (13, zr.at[pl.ds(0, ZN - 1)]), (14, full.at[c, y, x, three]), (15, full.at[c]),
    ):
        total_wait(ref, ssem.at[s])


def finish(f_any, zone_any, zg_ref, gin_ref, gmid_ref, gout_ref, gbias_ref, f_ref, zone_ref, sem):
    dest = lax.axis_index("dest")
    loads = [pltpu.make_async_copy(f_any.at[h], f_ref.at[h], sem.at[h]) for h in range(2)]
    loads.append(pltpu.make_async_copy(zone_any, zone_ref, sem.at[2]))
    for cp in loads:
        cp.start()
    for h in range(2):
        loads[h].wait()
        span = slice(h * 128, (h + 1) * 128)
        for q in range(16):
            for p in range(4):
                r = q * 16 + (p % 2) * 8
                gmid_ref[1 - p // 2, r : r + 8, span] = f_ref[h, q // 4, q % 4, p, 0:8]
        small = f_ref[h, :, :, :, 8, :].reshape(64, 128)
        gin_ref[0:FZ, span] = small[32 : 32 + FZ]
        gin_ref[FZ : 2 * FZ + 1, span] = small[0 : FZ + 1]
        gbias_ref[0:1, span] = small[20:21]
        gbias_ref[1:3, span] = small[24:26]
        gout_ref[0:1, span] = small[26:27]
        if h == 0:
            atm = small[28:32]
    table = jnp.concatenate(
        [jnp.concatenate([atm[:, o * 32 : (o + 1) * 32], jnp.zeros((4, 32), F32)], axis=0) for o in range(OA)],
        axis=0,
    )
    hits = (table[:, 20:21] == (iota((32, NZ), 1) + dest * NZ).astype(F32)).astype(F32)
    added = lax.dot_general(
        table, hits, (((0,), (0,)), ((), ())), preferred_element_type=F32, precision=lax.Precision.HIGHEST
    )
    loads[2].wait()
    for j in range(YN):
        span = slice(j * 128, (j + 1) * 128)
        zg_ref[:, span] = zone_ref[j, 0:FZ] + added[0:FZ, span]


def per_device(zone_feat, anchor_zone, distance, prior, flows, w_in, w_mid, w_out, biases):
    vm = pltpu.VMEM
    dma = pltpu.SemaphoreType.DMA
    def place(array, row, lane):
        rows, lanes = array.shape
        return lax.pad(array, BF16(0), ((row, 80 - row - rows, 0), (lane, NZ - lane - lanes, 0)))

    packed = place(zone_feat, 0, 0) + place(distance, 24, 0) + place(w_in, 32, 0) + place(biases, 72, 0)
    last = lax.pad(w_out, BF16(0), ((0, NZ - H, 0),))
    packed = packed + jnp.where(iota((80, NZ), 0) == 79, last[None, :], BF16(0))
    shapes = [
        vm((80, NZ), BF16), pltpu.SMEM((OA,), jnp.int32), vm((OA, NZ), F32), vm((OA, NZ), jnp.int32), vm((2, H, H), BF16),
        vm((32, H), BF16), vm((128, H), BF16), vm((2, H, H), BF16), vm((64, PAIRS), BF16),
        vm((OA, NZ, H), F32), vm((OA, NZ, H), BF16), vm((OA, NZ, H), BF16), vm((OA, NZ, H), BF16),
        vm((H + 16, PAIRS), BF16), vm((H + 16, PAIRS), BF16),
        vm((OA, NZ, H), F32), vm((OA, NZ, H), F32), vm((OA, NZ, H), F32),
        vm((PAIRS, H), BF16), vm((PAIRS, H), BF16), vm((PAIRS, H), BF16), vm((OA, 16, NZ), F32),
        vm((1, 128), F32), vm((XN * ZN, 1, 128), F32), vm((2, 8, 128), F32),
        vm((1, 128), F32), vm((XN * ZN, 1, 128), F32), vm((2, 8, 128), F32),
        vm((2, H, 128), F32), vm((2, H + 64, 128), F32), vm((H, 128), F32), vm((H + 64, 128), F32),
        vm((16, 16, 128), F32), vm((16, 20, 128), F32), vm((16, 16, 128), F32), vm((16, 20, 128), F32),
        vm((4, 9, 128), F32), vm((ZN, 9, 128), F32), vm((9, 128), F32), vm((2, YN, XN, 4, 9, 128), F32),
        vm((YN, 24, 128), F32), vm((YN, 24, 128), F32), vm((24, 128), F32), vm((YN, 24, 128), F32),
        dma((5,)), dma((17,)), dma((17,)), dma((4,)), dma((4,)), dma((2 * YN + 1,)), dma((4,)),
    ]
    vspec = pl.BlockSpec(memory_space=pltpu.VMEM)
    anyspec = pl.BlockSpec(memory_space=pl.ANY)
    zone, parts = pl.pallas_call(
        kernel,
        out_shape=(
            jax.ShapeDtypeStruct((YN, 24, 128), F32),
            jax.ShapeDtypeStruct((2, YN, XN, 4, 9, 128), F32),
        ),
        in_specs=[anyspec] * 5,
        out_specs=[anyspec] * 2,
        scratch_shapes=shapes,
        compiler_params=pltpu.CompilerParams(
            collective_id=0, has_side_effects=True, vmem_limit_bytes=60 * 2**20
        ),
        name="gravity_backward",
    )(packed, anchor_zone, prior, flows, w_mid)
    out = pl.pallas_call(
        finish,
        out_shape=(
            jax.ShapeDtypeStruct((FZ, NZ), F32),
            jax.ShapeDtypeStruct((2 * FZ + 1, H), F32),
            jax.ShapeDtypeStruct((2, H, H), F32),
            jax.ShapeDtypeStruct((1, H), F32),
            jax.ShapeDtypeStruct((3, H), F32),
        ),
        in_specs=[anyspec] * 2,
        out_specs=[vspec] * 5,
        scratch_shapes=[vm((2, YN, XN, 4, 9, 128), F32), vm((YN, 24, 128), F32), dma((3,))],
        name="results",
    )(parts, zone)
    return out[0], out[1], out[2], out[3].reshape(H), out[4]


def solution(mesh):
    in_specs = (
        P(None, "dest"), P("orig"), P("orig", "dest"), P("orig", "dest"), P("orig", "dest"), P(), P(), P(), P(),
    )
    out_specs = (P(None, "dest"), P(), P(), P(), P())
    return jax.shard_map(
        per_device, mesh=mesh, in_specs=in_specs, out_specs=out_specs, check_vma=False
    )
```
